32 devices in a mesh: grp: 2 (over y), band: 8 (over z, x), ch: 2 (over core).
Axes of the slice: x: 2, y: 2, z: 4, core: 2. Of those that a mesh axis runs over, the one named last changes fastest.
Arguments:
- grid_input: bfloat16 [32768, 227], P(('grp', 'band')), parts along dimension 0, may hold values from -6 to 6
- grid_senders: int32 [2048, 32], P(('grp', 'band')), parts along dimension 0, may hold values from 0 to 16383, as said below
- grid_lengths: int32 [2048], P(('grp', 'band')), parts along dimension 0, may hold values from 11 to 32, as said below
- grid_feats: bfloat16 [4, 65536], P(None, ('grp', 'band')), parts along dimension 1, may hold values from -6 to 6
- mesh_latent: bfloat16 [2048, 512], P(('grp', 'band'), 'ch'), parts along dimension 0, may hold values from -6 to 6
- mesh_senders: int32 [128, 16], P(('grp', 'band')), parts along dimension 0, may hold values from 0 to 127, as said below
- mesh_receivers: int32 [128, 16], P(('grp', 'band')), parts along dimension 0, may hold values from 0 to 127, as said below
- mesh_counts: int32 [16, 8], P(('grp', 'band')), parts along dimension 0, may hold values from 0 to 16, as said below
- mesh_feats: bfloat16 [4, 2048], P(None, ('grp', 'band')), parts along dimension 1, may hold values from -6 to 6
- embed_first: bfloat16 [227, 512], P(None, 'ch'), may hold values from -0.375 to 0.375
- embed_second: bfloat16 [512, 512], P('ch'), may hold values from -0.25 to 0.25
- link_sender: bfloat16 [512, 512], P(None, 'ch'), may hold values from -0.25 to 0.25
- link_receiver: bfloat16 [512, 512], P(None, 'ch'), may hold values from -0.25 to 0.25
- link_edge: bfloat16 [4, 512], P(None, 'ch'), may hold values from -3 to 3
- link_out: bfloat16 [512, 512], P('ch'), may hold values from -0.046875 to 0.046875
- proc_sender: bfloat16 [512, 512], P(None, 'ch'), may hold values from -0.25 to 0.25
- proc_receiver: bfloat16 [512, 512], P(None, 'ch'), may hold values from -0.25 to 0.25
- proc_edge: bfloat16 [4, 512], P(None, 'ch'), may hold values from -3 to 3
- proc_out: bfloat16 [512, 512], P('ch'), may hold values from -0.25 to 0.25
- node_first: bfloat16 [1024, 512], P(None, 'ch'), may hold values from -0.1875 to 0.1875
- node_second: bfloat16 [512, 512], P('ch'), may hold values from -0.25 to 0.25
- norm_gain: float32 [512], P('ch'), may hold values from 0.4 to 1.6
Outputs:
- mesh_out: bfloat16 [2048, 512], P(('grp', 'band'), 'ch'), parts along dimension 0
The draws below stay inside these ranges and needn't reach their ends.
There are 2 independent parts, one for each index of `grp`. The reference program is written for one: setup_inputs(seed, part) draws one part's arguments, and reference() takes and returns one part's arrays. A program takes and returns all parts, laid end to end along the dimension named above; an argument that names none is the same for every part. Nothing has to cross between parts.
Inputs may be any that keep to these rules, and one draw needn't show every extreme that they name: `grid_senders`: the senders of the mesh nodes of patch b (rows b * 128 to b * 128 + 127) lie in the latitude slabs b - 1, b, b + 1 (grid rows of slab q: q * 2048 to q * 2048 + 2047), within the grid. `grid_lengths`: each patch has at least one mesh node with all 32 slots used. `mesh_counts`: entry (b, p) is 0 unless p is b - 1, b or b + 1 modulo 8 (neighbouring patches) or p < 2 (patches that hold the coarse mesh levels); Each row has at least one block with all 16 slots used, from a neighbouring patch. `mesh_senders`: in a block from a patch p < 2 that is not a neighbour of b, the senders are coarse-level nodes: at most 4 distinct nodes of patch p, the same for every such block from p. `mesh_receivers`: in a block from a patch p < 2 that is not a neighbour of b, the receivers are coarse-level nodes: at most 4 distinct nodes of patch b, the same for every such block into b.
All inputs are finite; a program needn't handle non-finite values.
Results may differ from the reference program's by a relative error of at most 0.007.
Values may be sent and summed in bfloat16 or wider, within the bound.
No kernel may reach another device: no remote copies, remote signals or barrier semaphores. Data moves between devices by JAX's collectives and lax.ppermute only.
A program may use at most 64 MiB of HBM per device.

```python
import jax
import jax.numpy as jnp
from jax import lax

D = 512
CIN = 227
EF = 4
SLOTS = 32
COARSE = 2
G_DEV = 2048
M_DEV = 128
CAP = 16
G = 16384
M = 1024
N_BAND = 8
N_CH = 2


def coarse_nodes(key):
    node_key = jax.random.fold_in(key, 5)
    return jax.random.randint(node_key, (N_BAND, 4), 0, M_DEV, dtype=jnp.int32)


def far_rows():
    rows = jnp.arange(N_BAND * N_BAND, dtype=jnp.int32)
    receiver_patch = rows // N_BAND
    sender_patch = rows % N_BAND
    distance = (sender_patch - receiver_patch + 1) % N_BAND
    is_far = (sender_patch < COARSE) & (distance >= 3)
    return (receiver_patch, sender_patch, is_far)


def draw_grid_senders(key, part):
    key = jax.random.fold_in(key, 11)
    first_key, second_key = jax.random.split(key)
    patch_of = (jnp.arange(M, dtype=jnp.int32) // M_DEV)[:, None]
    offset = jax.random.randint(first_key, (M, SLOTS), -1, 2, dtype=jnp.int32)
    owner_slab = jnp.clip(patch_of + offset, 0, N_BAND - 1)
    row_within = jax.random.randint(second_key, (M, SLOTS), 0, G_DEV, dtype=jnp.int32)
    return (owner_slab * G_DEV + row_within).astype(jnp.int32)


def draw_grid_lengths(key, part):
    key = jax.random.fold_in(key, 23)
    first_key, second_key = jax.random.split(key)
    lengths = jax.random.randint(first_key, (M,), SLOTS // 3 + 1, SLOTS + 1, dtype=jnp.int32)
    chosen = jax.random.randint(second_key, (N_BAND,), 0, M_DEV, dtype=jnp.int32)
    node_index = jnp.arange(M, dtype=jnp.int32)
    is_full = node_index % M_DEV == chosen[node_index // M_DEV]
    return jnp.where(is_full, SLOTS, lengths).astype(jnp.int32)


def draw_mesh_senders(key, part):
    nodes = coarse_nodes(key)
    key = jax.random.fold_in(key, 41)
    drawn_key, pick_key = jax.random.split(key)
    receiver_patch, sender_patch, is_far = far_rows()
    drawn = jax.random.randint(drawn_key, (N_BAND * N_BAND, CAP), 0, M_DEV, dtype=jnp.int32)
    pick = jax.random.randint(pick_key, (N_BAND * N_BAND, CAP), 0, 4, dtype=jnp.int32)
    coarse = jnp.take_along_axis(nodes[sender_patch], pick, axis=1)
    return jnp.where(is_far[:, None], coarse, drawn).astype(jnp.int32)


def draw_mesh_receivers(key, part):
    nodes = coarse_nodes(key)
    key = jax.random.fold_in(key, 53)
    drawn_key, pick_key = jax.random.split(key)
    receiver_patch, sender_patch, is_far = far_rows()
    drawn = jax.random.randint(drawn_key, (N_BAND * N_BAND, CAP), 0, M_DEV, dtype=jnp.int32)
    pick = jax.random.randint(pick_key, (N_BAND * N_BAND, CAP), 0, 4, dtype=jnp.int32)
    coarse = jnp.take_along_axis(nodes[receiver_patch], pick, axis=1)
    return jnp.where(is_far[:, None], coarse, drawn).astype(jnp.int32)


def draw_mesh_counts(key, part):
    key = jax.random.fold_in(key, 37)
    near_key, far_key, full_key = jax.random.split(key, 3)
    receiver_patch = jnp.arange(N_BAND, dtype=jnp.int32)[:, None]
    sender_patch = jnp.arange(N_BAND, dtype=jnp.int32)[None, :]
    distance = (sender_patch - receiver_patch + 1) % N_BAND
    is_near = distance < 3
    is_far = (sender_patch < COARSE) & jnp.logical_not(is_near)
    near_counts = jax.random.randint(near_key, (N_BAND, N_BAND), CAP // 2, CAP + 1, dtype=jnp.int32)
    far_counts = jax.random.randint(far_key, (N_BAND, N_BAND), CAP // 2, CAP + 1, dtype=jnp.int32)
    chosen = jax.random.randint(full_key, (N_BAND, 1), 0, 3, dtype=jnp.int32)
    near_counts = jnp.where(distance == chosen, CAP, near_counts)
    counts = jnp.where(is_near, near_counts, jnp.where(is_far, far_counts, 0))
    return counts.astype(jnp.int32)


def steps_of(stream_key, extent, cuts, smallest, top_value):
    gain = 1.0
    for axis_at, parts in cuts:
        steps = jax.random.uniform(jax.random.fold_in(jax.random.fold_in(stream_key, 6), axis_at), (parts,), jnp.float32, smallest / len(cuts), top_value / len(cuts))
        gain = gain * jnp.repeat(jnp.exp(steps), extent[axis_at] // parts).reshape((-1,) + (1,) * (len(extent) - 1 - axis_at))
    return gain


def bell_draw(key, dims, spread, reach, cuts=(), kind=jnp.bfloat16):
    values = spread * jax.random.normal(key, dims, jnp.float32)
    if cuts:
        values = values * steps_of(key, dims, cuts, -0.22, 0.18)
    return jnp.clip(values, -reach, reach).astype(kind)


def setup_inputs(seed: int = 0, part: int = 0) -> dict:
    arg_keys = jax.random.split(jax.random.key(seed), 23)
    part_splits = jax.random.split(jax.random.fold_in(arg_keys[22], part), 23)
    grid_input = bell_draw(part_splits[0], (G, CIN), 1.0, 6.0, ((0, 8),))
    grid_senders = draw_grid_senders(jax.random.fold_in(jax.random.fold_in(arg_keys[22], part), 71), part)
    grid_lengths = draw_grid_lengths(jax.random.fold_in(jax.random.fold_in(arg_keys[22], part), 71), part)
    grid_feats = bell_draw(part_splits[3], (EF, M * SLOTS), 1.0, 6.0, ((1, 8),))
    mesh_latent = bell_draw(part_splits[4], (M, D), 1.0, 6.0, ((0, 8), (1, 2)))
    mesh_senders = draw_mesh_senders(jax.random.fold_in(jax.random.fold_in(arg_keys[22], part), 71), part)
    mesh_receivers = draw_mesh_receivers(jax.random.fold_in(jax.random.fold_in(arg_keys[22], part), 71), part)
    mesh_counts = draw_mesh_counts(jax.random.fold_in(jax.random.fold_in(arg_keys[22], part), 71), part)
    mesh_feats = bell_draw(part_splits[8], (EF, N_BAND * N_BAND * CAP), 1.0, 6.0, ((1, 8),))
    embed_first = bell_draw(arg_keys[9], (CIN, D), CIN ** -0.5, 0.375, ((1, 2),))
    embed_second = bell_draw(arg_keys[10], (D, D), D ** -0.5, 0.25, ((0, 2),))
    link_sender = bell_draw(arg_keys[11], (D, D), D ** -0.5, 0.25, ((1, 2),))
    link_receiver = bell_draw(arg_keys[12], (D, D), D ** -0.5, 0.25, ((1, 2),))
    link_edge = bell_draw(arg_keys[13], (EF, D), EF ** -0.5, 3.0, ((1, 2),))
    link_out = bell_draw(arg_keys[14], (D, D), (D * SLOTS) ** -0.5, 0.046875, ((0, 2),))
    proc_sender = bell_draw(arg_keys[15], (D, D), D ** -0.5, 0.25, ((1, 2),))
    proc_receiver = bell_draw(arg_keys[16], (D, D), D ** -0.5, 0.25, ((1, 2),))
    proc_edge = bell_draw(arg_keys[17], (EF, D), EF ** -0.5, 3.0, ((1, 2),))
    proc_out = bell_draw(arg_keys[18], (D, D), D ** -0.5, 0.25, ((0, 2),))
    node_first = bell_draw(arg_keys[19], (2 * D, D), (2 * D) ** -0.5, 0.1875, ((1, 2),))
    node_second = bell_draw(arg_keys[20], (D, D), D ** -0.5, 0.25, ((0, 2),))
    norm_gain = jnp.clip(1.0 + 0.12 * jax.random.normal(arg_keys[21], (D,), jnp.float32), 0.4, 1.6)
    return dict(grid_input=grid_input, grid_senders=grid_senders, grid_lengths=grid_lengths, grid_feats=grid_feats, mesh_latent=mesh_latent, mesh_senders=mesh_senders, mesh_receivers=mesh_receivers, mesh_counts=mesh_counts, mesh_feats=mesh_feats, embed_first=embed_first, embed_second=embed_second, link_sender=link_sender, link_receiver=link_receiver, link_edge=link_edge, link_out=link_out, proc_sender=proc_sender, proc_receiver=proc_receiver, proc_edge=proc_edge, proc_out=proc_out, node_first=node_first, node_second=node_second, norm_gain=norm_gain)


def reference(grid_input, grid_senders, grid_lengths, grid_feats, mesh_latent, mesh_senders, mesh_receivers, mesh_counts, mesh_feats, embed_first, embed_second, link_sender, link_receiver, link_edge, link_out, proc_sender, proc_receiver, proc_edge, proc_out, node_first, node_second, norm_gain):
    embed_hidden = jax.nn.silu(jnp.dot(grid_input, embed_first, preferred_element_type=jnp.float32)).astype(jnp.bfloat16)
    block_width = D // N_CH
    latent_total = jnp.zeros((G, D), jnp.float32)
    for block_index in range(N_CH):
        lower = block_index * block_width
        piece_sum = jnp.dot(embed_hidden[:, lower:lower + block_width], embed_second[lower:lower + block_width], preferred_element_type=jnp.float32).astype(jnp.bfloat16)
        piece_sum = lax.optimization_barrier(piece_sum)
        latent_total = latent_total + piece_sum.astype(jnp.float32)
    grid_latent = latent_total.astype(jnp.bfloat16)
    grid_send = jnp.dot(grid_latent, link_sender, preferred_element_type=jnp.float32).astype(jnp.bfloat16)
    mesh_recv_term = jnp.dot(mesh_latent, link_receiver, preferred_element_type=jnp.float32)

    def link_block(patch):
        first = (patch * M_DEV).astype(jnp.int32)
        senders = lax.dynamic_slice_in_dim(grid_senders, first, M_DEV, 0)
        lengths = lax.dynamic_slice_in_dim(grid_lengths, first, M_DEV, 0)
        sender_rows = grid_send[senders.reshape(-1)].astype(jnp.float32).reshape(M_DEV, SLOTS, D)
        features = lax.dynamic_slice_in_dim(grid_feats, (first * SLOTS).astype(jnp.int32), M_DEV * SLOTS, 1)
        edge_term = jnp.einsum('ce,cd->ed', features.astype(jnp.float32), link_edge.astype(jnp.float32)).reshape(M_DEV, SLOTS, D)
        receiver_term = lax.dynamic_slice_in_dim(mesh_recv_term, first, M_DEV, 0)
        activity = jax.nn.silu(sender_rows + receiver_term[:, None, :] + edge_term)
        valid = jnp.arange(SLOTS, dtype=jnp.int32)[None, :] < lengths[:, None]
        return lax.optimization_barrier(jnp.sum(jnp.where(valid[:, :, None], activity, jnp.float32(0.0)), axis=1)).astype(jnp.bfloat16)
    link_pool = lax.map(link_block, jnp.arange(N_BAND, dtype=jnp.int32)).reshape(M, D)
    mesh_mid = (mesh_latent.astype(jnp.float32) + jnp.dot(link_pool, link_out, preferred_element_type=jnp.float32)).astype(jnp.bfloat16)
    mesh_send = jnp.dot(mesh_mid, proc_sender, preferred_element_type=jnp.float32).astype(jnp.bfloat16)
    mesh_recv = jnp.dot(mesh_mid, proc_receiver, preferred_element_type=jnp.float32)

    def proc_block(patch):
        first_row = (patch * N_BAND).astype(jnp.int32)
        senders = lax.dynamic_slice_in_dim(mesh_senders, first_row, N_BAND, 0)
        receivers = lax.dynamic_slice_in_dim(mesh_receivers, first_row, N_BAND, 0).reshape(-1)
        counts = lax.dynamic_slice_in_dim(mesh_counts, patch.astype(jnp.int32), 1, 0)[0]
        global_senders = (jnp.arange(N_BAND, dtype=jnp.int32)[:, None] * M_DEV + senders).reshape(-1)
        sender_rows = mesh_send[global_senders].astype(jnp.float32)
        receiver_block = lax.dynamic_slice_in_dim(mesh_recv, (patch * M_DEV).astype(jnp.int32), M_DEV, 0)
        receiver_term = receiver_block[receivers]
        features = lax.dynamic_slice_in_dim(mesh_feats, (first_row * CAP).astype(jnp.int32), N_BAND * CAP, 1)
        edge_term = jnp.einsum('ce,cd->ed', features.astype(jnp.float32), proc_edge.astype(jnp.float32))
        activity = jax.nn.silu(sender_rows + receiver_term + edge_term).astype(jnp.bfloat16)
        valid = (jnp.arange(CAP, dtype=jnp.int32)[None, :] < counts[:, None]).reshape(-1)
        masked = jnp.where(valid[:, None], activity.astype(jnp.float32), jnp.float32(0.0))
        return jax.ops.segment_sum(masked, receivers, num_segments=M_DEV).astype(jnp.bfloat16)
    proc_pool = lax.map(proc_block, jnp.arange(N_BAND, dtype=jnp.int32)).reshape(M, D)
    proc_agg = jnp.dot(proc_pool, proc_out, preferred_element_type=jnp.float32).astype(jnp.bfloat16)
    joined = jnp.concatenate([mesh_mid, proc_agg], axis=1)
    node_hidden = jax.nn.silu(jnp.dot(joined, node_first, preferred_element_type=jnp.float32)).astype(jnp.bfloat16)
    node_update = jnp.dot(node_hidden, node_second, preferred_element_type=jnp.float32)
    row_mean = lax.optimization_barrier(jnp.sum(node_update, axis=1)) / D
    row_square = lax.optimization_barrier(jnp.sum(node_update * node_update, axis=1)) / D
    row_var = row_square - row_mean * row_mean
    normed = (node_update - row_mean[:, None]) * lax.rsqrt(row_var + 1e-05)[:, None] * norm_gain[None, :]
    return (mesh_mid.astype(jnp.float32) + normed).astype(jnp.bfloat16)
```

```python
import functools

import jax
import jax.numpy as jnp
from jax import lax
from jax.experimental import pallas as pl
from jax.experimental.pallas import tpu as pltpu
from jax.sharding import PartitionSpec as P

F32 = jnp.float32
BF16 = jnp.bfloat16
LANES = 128
CHUNK = 256
BLOCKS_PER_GROUP = 8
VMEM_LIMIT = 48 * 1024 * 1024


def dot(a, b):
    return jnp.dot(a, b, preferred_element_type=F32)


def dot_on(a, b, dim_a, dim_b):
    return lax.dot_general(a, b, (((dim_a,), (dim_b,)), ((), ())), preferred_element_type=F32)


def silu(v):
    return 0.5 * v * (1.0 + jnp.tanh(0.5 * v))


def iota(shape, dim):
    return lax.broadcasted_iota(jnp.int32, shape, dim)


def ones_where(mask):
    return jnp.where(mask, 1.0, 0.0).astype(BF16)


def call(body, out_shape, args, grid_spec=None, flops=0, moved=0, scratch=(), **kw):
    whole = pl.BlockSpec(memory_space=pltpu.VMEM)
    if "in_specs" not in kw:
        kw["in_specs"] = [whole] * len(args)
        kw["out_specs"] = jax.tree.map(lambda _: whole, out_shape)
    return pl.pallas_call(
        body,
        out_shape=out_shape,
        scratch_shapes=list(scratch),
        compiler_params=pltpu.CompilerParams(vmem_limit_bytes=VMEM_LIMIT),
        cost_estimate=pl.CostEstimate(flops=flops, bytes_accessed=moved, transcendentals=0),
        **kw,
    )(*args)


def pack_body(slab_rows, senders_ref, lengths_ref, feats_ref, own_ref, other_ref, out_ref):
    band = lax.axis_index("band")
    core = lax.axis_index("ch")
    nodes, slots = senders_ref.shape
    width = out_ref.shape[1]
    own, other = own_ref[...], other_ref[...]
    first = core == 0
    out_ref[0:nodes, :] = jnp.concatenate(
        [jnp.where(first, own, other), jnp.where(first, other, own)], axis=1
    )
    per_row = LANES // slots
    rows = nodes // per_row
    pieces = [senders_ref[pl.ds(j, rows, stride=per_row), :] for j in range(per_row)]
    index = jnp.concatenate(pieces, axis=1) - (band - 1) * slab_rows
    shape = (rows, LANES)
    spread = jnp.where(
        iota((rows, nodes), 1) // per_row == iota((rows, nodes), 0),
        lengths_ref[...].astype(F32),
        0.0,
    ).astype(BF16)
    pick = ones_where(iota((nodes, LANES), 0) % per_row == iota((nodes, LANES), 1) // slots)
    length = dot(spread, pick)
    used = (iota(shape, 1) % slots).astype(F32) < length
    high = jnp.where(used, index // LANES + 1, 0).astype(F32)
    low = jnp.where(used, index % LANES, 0).astype(F32)
    fill = jnp.zeros((rows, width - 2 * LANES), F32)
    feats = feats_ref[...].astype(F32)
    parts = [feats[:, k * width : (k + 1) * width] for k in range(feats.shape[1] // width)]
    tail = jnp.concatenate(parts + [jnp.concatenate([high, low, fill], axis=1)], axis=0)
    out_ref[nodes:, :] = tail.astype(BF16)


def embed_body(x_ref, f_own, f_oth, s_own, s_oth, l_own, l_oth, out_ref):
    x = x_ref[...]
    half = f_own.shape[1]
    hidden_own = silu(dot(x, f_own[...])).astype(BF16)
    hidden_oth = silu(dot(x, f_oth[...])).astype(BF16)
    latent = (dot(hidden_own, s_own[...]) + dot(hidden_oth, s_oth[...])).astype(BF16)
    out_ref[:, :half] = dot(latent, l_own[...]).astype(BF16)
    out_ref[:, half:] = dot(latent, l_oth[...]).astype(BF16)


def pool_part(high, low, feats, latent, kind, slots, table_ref, weights, payload, ranks, right, out_ref):
    lr_own, lr_oth, le_own, le_oth = weights
    blocks = high.shape[0]
    nodes = latent.shape[0]
    groups = blocks // BLOCKS_PER_GROUP
    group_nodes = nodes // groups
    group_slots = BLOCKS_PER_GROUP * LANES
    table_rows, width = table_ref.shape
    per_slab = table_rows // LANES
    recv = jnp.concatenate([dot(latent, lr_own[...]), dot(latent, lr_oth[...])], axis=1)
    recv_high = recv.astype(BF16).astype(F32)
    recv_low = recv - recv_high
    edge = jnp.concatenate([le_own[...], le_oth[...]], axis=1).astype(F32)
    base = (kind * per_slab + 1).astype(F32)
    local = high - base
    valid = (local >= 0.0) & (local < float(per_slab))
    flag = jnp.where(valid, 1.0, 0.0)
    flag16 = flag.astype(BF16)
    inclusive = dot(flag16, ones_where(iota((LANES, LANES), 0) <= iota((LANES, LANES), 1)))
    square = (blocks, blocks)
    ahead = ones_where(
        (iota(square, 1) < iota(square, 0))
        & (iota(square, 1) // BLOCKS_PER_GROUP == iota(square, 0) // BLOCKS_PER_GROUP)
    )
    offset = jnp.sum(dot(ahead, flag16), axis=1, keepdims=True)
    ranks[...] = jnp.where(valid, inclusive - flag + offset, -1.0)
    out_ref[...] = jnp.zeros(out_ref.shape, F32)
    node_rows = jnp.where(
        iota((group_nodes, group_slots), 1) // slots == iota((group_nodes, group_slots), 0), 1.0, 0.0
    )
    for g in range(groups):
        at = g * BLOCKS_PER_GROUP
        row_high = jnp.concatenate(
            [local[at + k : at + k + 1, :] for k in range(BLOCKS_PER_GROUP)], axis=1
        )
        row_low = jnp.concatenate(
            [low[at + k : at + k + 1, :] for k in range(BLOCKS_PER_GROUP)], axis=1
        )
        payload[...] = jnp.concatenate(
            [
                feats[g],
                row_high,
                row_low,
                jnp.zeros((2, group_slots), F32),
                node_rows,
                node_rows,
                jnp.zeros((8, group_slots), F32),
            ],
            axis=0,
        ).astype(BF16)
        n0 = g * group_nodes
        right[...] = jnp.concatenate(
            [
                edge,
                jnp.zeros((4, width), F32),
                recv_high[n0 : n0 + group_nodes],
                recv_low[n0 : n0 + group_nodes],
                jnp.zeros((8, width), F32),
            ],
            axis=0,
        ).astype(BF16)
        count = jnp.sum(flag[at : at + BLOCKS_PER_GROUP]).astype(jnp.int32)

        @pl.loop(0, (count + CHUNK - 1) // CHUNK)
        def _(step):
            wanted = (iota((CHUNK, LANES), 0) + step * CHUNK).astype(F32)
            select = jnp.concatenate(
                [
                    ones_where(ranks[at + k : at + k + 1, :] == wanted)
                    for k in range(BLOCKS_PER_GROUP)
                ],
                axis=1,
            )
            compact = dot_on(select, payload[...], 1, 1)
            row = (compact[:, 4:5] * float(LANES) + compact[:, 5:6]).astype(jnp.int32)
            choose = ones_where(row == iota((CHUNK, table_rows), 1))
            compact = compact.astype(BF16)
            pre = dot(choose, table_ref[...]) + dot(compact, right[...])
            act = silu(pre).astype(BF16)
            out_ref[n0 : n0 + group_nodes, :] += dot_on(
                compact[:, 8 : 8 + group_nodes], act, 0, 0
            )


def unpack(packed_ref, nodes, slots):
    width = packed_ref.shape[1]
    blocks = nodes * slots // LANES
    tail = packed_ref[nodes:, :].astype(F32)
    feat_rows = tail.shape[0] - blocks
    high = tail[feat_rows:, 0:LANES]
    low = tail[feat_rows:, LANES : 2 * LANES]
    per_group = BLOCKS_PER_GROUP * LANES // width
    feats = []
    for g in range(blocks // BLOCKS_PER_GROUP):
        rows = [tail[4 * k : 4 * k + 4] for k in range(g * per_group, (g + 1) * per_group)]
        feats.append(jnp.concatenate(rows, axis=1))
    return high, low, feats


def own_pool_body(nodes, slots, packed_ref, table_ref, lr_own, lr_oth, le_own, le_oth, out_ref, payload, ranks, right):
    first = lax.axis_index("ch") == 0
    high, low, feats = unpack(packed_ref, nodes, slots)
    half_blocks = high.shape[0] // 2
    half_groups = len(feats) // 2
    pick = lambda a, b: jnp.where(first, a, b)
    latent = pick(packed_ref[0 : nodes // 2, :], packed_ref[nodes // 2 : nodes, :])
    pool_part(
        pick(high[:half_blocks], high[half_blocks:]),
        pick(low[:half_blocks], low[half_blocks:]),
        [pick(feats[k], feats[half_groups + k]) for k in range(half_groups)],
        latent,
        jnp.int32(1),
        slots,
        table_ref,
        (lr_own, lr_oth, le_own, le_oth),
        payload,
        ranks,
        right,
        out_ref,
    )


def near_pool_body(nodes, slots, packed_ref, table_ref, lr_own, lr_oth, le_own, le_oth, out_ref, payload, ranks, right, total):
    high, low, feats = unpack(packed_ref, nodes, slots)
    kind = 2 * lax.axis_index("ch")
    pool_part(
        high,
        low,
        feats,
        packed_ref[0:nodes, :],
        kind,
        slots,
        table_ref,
        (lr_own, lr_oth, le_own, le_oth),
        payload,
        ranks,
        right,
        total,
    )
    out_ref[...] = total[...].astype(BF16)


def middle_body(packed_ref, near_ref, near_oth_ref, own_ref, own_oth_ref, lo_own, lo_oth, ps, pr, mid_ref, send_ref, recv_ref):
    first = lax.axis_index("ch") == 0
    half = lo_own.shape[0]
    nodes = near_ref.shape[0]
    mine, theirs = own_ref[...], own_oth_ref[...]
    flip = lambda a: jnp.concatenate([a[:, half:], a[:, :half]], axis=1)
    theirs = flip(theirs)
    total = near_ref[...].astype(F32) + flip(near_oth_ref[...]).astype(F32)
    total = total + jnp.concatenate(
        [jnp.where(first, mine, theirs), jnp.where(first, theirs, mine)], axis=0
    )
    pool = total.astype(BF16)
    agg = dot(pool[:, :half], lo_own[...]) + dot(pool[:, half:], lo_oth[...])
    mid = (packed_ref[0:nodes, :].astype(F32) + agg).astype(BF16)
    mid_ref[...] = mid
    send_ref[...] = dot(mid, ps[...]).astype(BF16)
    recv_ref[...] = dot(mid, pr[...])


def edge_body(patches, piece_ref, recv_ref, senders_ref, receivers_ref, limit_ref, feats_ref, pe, pool_ref):
    nodes = recv_ref.shape[0]
    rows = patches * nodes
    slots = senders_ref.shape[1] * rows // piece_ref.shape[0]
    recv = recv_ref[...]
    recv_high = recv.astype(BF16)
    recv_low = (recv - recv_high.astype(F32)).astype(BF16)
    total = None
    for k in range(piece_ref.shape[0] // rows):
        lanes = slice(k * slots, (k + 1) * slots)
        patch = iota((1, slots), 1) // (slots // patches)
        choose = ones_where(iota((rows, slots), 0) == senders_ref[:, lanes] + patch * nodes)
        into = iota((nodes, slots), 0) == receivers_ref[:, lanes]
        into16 = ones_where(into)
        pre = (
            dot_on(choose, piece_ref[k * rows : (k + 1) * rows, :], 0, 0)
            + dot_on(into16, recv_high, 0, 0)
            + dot_on(into16, recv_low, 0, 0)
            + dot_on(feats_ref[:, lanes], pe[...], 0, 0)
        )
        act = silu(pre).astype(BF16)
        part = dot(ones_where(into & (limit_ref[:, lanes] > 0)), act)
        total = part if total is None else total + part
    pool_ref[...] = total.astype(BF16)


def node_body(mid_ref, pool_ref, pool_oth_ref, po_own, po_oth, nf_own, nf_oth, ns_own, ns_oth, gain_ref, out_ref):
    first = lax.axis_index("ch") == 0
    width = mid_ref.shape[1]
    half = width // 2
    mid = mid_ref[...]
    agg = (dot(pool_ref[...], po_own[...]) + dot(pool_oth_ref[...], po_oth[...])).astype(BF16)
    update = None
    for nf, ns in ((nf_own, ns_own), (nf_oth, ns_oth)):
        hidden = silu(dot(mid, nf[0:width, :]) + dot(agg, nf[width:, :])).astype(BF16)
        term = dot(hidden, ns[...])
        update = term if update is None else update + term
    mean = jnp.sum(update, axis=1, keepdims=True) / width
    square = jnp.sum(update * update, axis=1, keepdims=True) / width
    scale = lax.rsqrt(square - mean * mean + 1e-05)
    pick = lambda a: jnp.where(first, a[:, :half], a[:, half:])
    out_ref[...] = (
        pick(mid).astype(F32) + (pick(update) - mean) * scale * gain_ref[...]
    ).astype(BF16)


def per_device(
    grid_input,
    grid_senders,
    grid_lengths,
    grid_feats,
    mesh_latent,
    mesh_senders,
    mesh_receivers,
    mesh_counts,
    mesh_feats,
    embed_first,
    embed_second,
    link_sender,
    link_receiver,
    link_edge,
    link_out,
    proc_sender,
    proc_receiver,
    proc_edge,
    proc_out,
    node_first,
    node_second,
    norm_gain,
):
    bands = lax.axis_size("band")
    slab_rows = grid_input.shape[0]
    nodes, slots = grid_senders.shape
    half = link_sender.shape[1]
    width = 2 * half
    capacity = mesh_senders.shape[1]
    edges = bands * capacity
    other = lambda a: lax.ppermute(a, "ch", [(0, 1), (1, 0)])
    at = lambda b, c: 2 * b + c
    to_owner = [(at(b + 1, 0), at(b, 0)) for b in range(bands - 1)]
    to_owner += [(at(b, 1), at(b + 1, 1)) for b in range(bands - 1)]
    to_patch = [(d, s) for s, d in to_owner]
    shape = jax.ShapeDtypeStruct

    latent_other = other(mesh_latent)
    packed_rows = nodes + 4 * (nodes * slots // width) + nodes * slots // LANES
    packed = call(
        functools.partial(pack_body, slab_rows),
        shape((packed_rows, width), BF16),
        (grid_senders, grid_lengths.reshape(1, nodes), grid_feats, mesh_latent, latent_other),
    )
    near_packed = lax.ppermute(packed, ("band", "ch"), to_owner)

    tile = slab_rows // 4
    fixed = lambda a: pl.BlockSpec(a.shape, lambda i: (0, 0))
    embed_weights = []
    for w in (embed_first, embed_second, link_sender):
        embed_weights += [w, other(w)]
    table = call(
        embed_body,
        shape((slab_rows, width), BF16),
        (grid_input, *embed_weights),
        grid=(slab_rows // tile,),
        in_specs=[pl.BlockSpec((tile, grid_input.shape[1]), lambda i: (i, 0))]
        + [fixed(w) for w in embed_weights],
        out_specs=pl.BlockSpec((tile, width), lambda i: (i, 0)),
        flops=2 * slab_rows * width * (256 + 2 * width),
        moved=4 * 1024 * 1024,
    )

    link_weights = (link_receiver, other(link_receiver), link_edge, other(link_edge))
    group_slots = BLOCKS_PER_GROUP * LANES
    group_nodes = group_slots // slots
    blocks = nodes * slots // LANES
    scratch = lambda count: [
        pltpu.VMEM((16 + 2 * group_nodes, group_slots), BF16),
        pltpu.VMEM((count, LANES), F32),
        pltpu.VMEM((16 + 2 * group_nodes, width), BF16),
    ]
    own = call(
        functools.partial(own_pool_body, nodes, slots),
        shape((nodes // 2, width), F32),
        (packed, table, *link_weights),
        scratch=scratch(blocks // 2),
        flops=4 * 10**9,
        moved=4 * 1024 * 1024,
    )
    own_other = other(own)
    near = call(
        functools.partial(near_pool_body, nodes, slots),
        shape((nodes, width), BF16),
        (near_packed, table, *link_weights),
        scratch=scratch(blocks) + [pltpu.VMEM((nodes, width), F32)],
        flops=4 * 10**9,
        moved=4 * 1024 * 1024,
    )
    near_back = lax.ppermute(near, ("band", "ch"), to_patch)
    near_back_other = other(near_back)

    mid, send, recv = call(
        middle_body,
        (shape((nodes, width), BF16), shape((nodes, half), BF16), shape((nodes, half), F32)),
        (packed, near_back, near_back_other, own, own_other, link_out, other(link_out), proc_sender, proc_receiver),
    )
    spread = jnp.broadcast_to(send[None], (bands, nodes, half)).reshape(bands * nodes, half)
    piece = lax.all_to_all(spread, "band", 0, 0, tiled=True)

    limit = (
        mesh_counts.reshape(bands, 1) - jnp.arange(capacity, dtype=jnp.int32)[None, :]
    ).reshape(1, edges)
    pool = call(
        functools.partial(edge_body, LANES // capacity),
        shape((nodes, half), BF16),
        (piece, recv, mesh_senders.reshape(1, edges), mesh_receivers.reshape(1, edges), limit, mesh_feats, proc_edge),
    )
    return call(
        node_body,
        shape((nodes, half), BF16),
        (
            mid,
            pool,
            other(pool),
            proc_out,
            other(proc_out),
            node_first,
            other(node_first),
            node_second,
            other(node_second),
            norm_gain.reshape(1, half),
        ),
    )


def solution(mesh):
    rows = P(("grp", "band"), None)
    columns = P(None, ("grp", "band"))
    split = P(("grp", "band"), "ch")
    by_column = P(None, "ch")
    by_row = P("ch", None)
    in_specs = (
        rows,
        rows,
        P(("grp", "band")),
        columns,
        split,
        rows,
        rows,
        rows,
        columns,
        by_column,
        by_row,
        by_column,
        by_column,
        by_column,
        by_row,
        by_column,
        by_column,
        by_column,
        by_row,
        by_column,
        by_row,
        P("ch"),
    )
    return jax.shard_map(
        per_device, mesh=mesh, in_specs=in_specs, out_specs=split, check_vma=False
    )
```

```python
import functools

import jax
import jax.numpy as jnp
from jax import lax
from jax.experimental import pallas as pl
from jax.experimental.pallas import tpu as pltpu
from jax.sharding import PartitionSpec as P

F32 = jnp.float32
BF16 = jnp.bfloat16
LANES = 128
CHUNK = 288
BLOCKS_PER_GROUP = 8
VMEM_LIMIT = 48 * 1024 * 1024


def dot(a, b):
    return jnp.dot(a, b, preferred_element_type=F32)


def dot_on(a, b, dim_a, dim_b):
    return lax.dot_general(a, b, (((dim_a,), (dim_b,)), ((), ())), preferred_element_type=F32)


def silu(v):
    return 0.5 * v * (1.0 + jnp.tanh(0.5 * v))


def iota(shape, dim):
    return lax.broadcasted_iota(jnp.int32, shape, dim)


def ones_where(mask):
    return jnp.where(mask, 1.0, 0.0).astype(BF16)


def call(body, out_shape, args, grid_spec=None, flops=0, moved=0, scratch=(), **kw):
    whole = pl.BlockSpec(memory_space=pltpu.VMEM)
    if "in_specs" not in kw:
        kw["in_specs"] = [whole] * len(args)
        kw["out_specs"] = jax.tree.map(lambda _: whole, out_shape)
    return pl.pallas_call(
        body,
        out_shape=out_shape,
        scratch_shapes=list(scratch),
        compiler_params=pltpu.CompilerParams(vmem_limit_bytes=VMEM_LIMIT),
        cost_estimate=pl.CostEstimate(flops=flops, bytes_accessed=moved, transcendentals=0),
        **kw,
    )(*args)


def pack_body(slab_rows, senders_ref, lengths_ref, feats_ref, own_ref, other_ref, out_ref, turned):
    band = lax.axis_index("band")
    core = lax.axis_index("ch")
    slots, nodes = senders_ref.shape
    width = out_ref.shape[1]
    turned[...] = (senders_ref[...] - (band - 1) * slab_rows).astype(F32).T
    own, other = own_ref[...], other_ref[...]
    first = core == 0
    out_ref[0:nodes, :] = jnp.concatenate(
        [jnp.where(first, own, other), jnp.where(first, other, own)], axis=1
    )
    per_row = LANES // slots
    rows = nodes // per_row
    pieces = [turned[pl.ds(j, rows, stride=per_row), :] for j in range(per_row)]
    index = jnp.concatenate(pieces, axis=1).astype(jnp.int32)
    shape = (rows, LANES)
    spread = jnp.where(
        iota((rows, nodes), 1) // per_row == iota((rows, nodes), 0),
        lengths_ref[...].astype(F32),
        0.0,
    ).astype(BF16)
    pick = ones_where(iota((nodes, LANES), 0) % per_row == iota((nodes, LANES), 1) // slots)
    length = dot(spread, pick)
    used = (iota(shape, 1) % slots).astype(F32) < length
    high = jnp.where(used, index // LANES + 1, 0).astype(F32)
    low = jnp.where(used, index % LANES, 0).astype(F32)
    fill = jnp.zeros((rows, width - 2 * LANES), F32)
    feats = feats_ref[...].astype(F32)
    parts = [feats[:, k * width : (k + 1) * width] for k in range(feats.shape[1] // width)]
    tail = jnp.concatenate(parts + [jnp.concatenate([high, low, fill], axis=1)], axis=0)
    out_ref[nodes:, :] = tail.astype(BF16)


def embed_body(x_ref, f_own, f_oth, s_own, s_oth, l_own, l_oth, out_ref):
    x = x_ref[...]
    half = f_own.shape[1]
    hidden_own = silu(dot_on(x, f_own[...], 0, 0)).astype(BF16)
    hidden_oth = silu(dot_on(x, f_oth[...], 0, 0)).astype(BF16)
    latent = (dot(hidden_own, s_own[...]) + dot(hidden_oth, s_oth[...])).astype(BF16)
    out_ref[:, :half] = dot(latent, l_own[...]).astype(BF16)
    out_ref[:, half:] = dot(latent, l_oth[...]).astype(BF16)


def pool_part(high, low, feats, latent, kind, slots, table_ref, weights, payload, ranks, right, out_ref):
    lr_own, lr_oth, le_own, le_oth = weights
    blocks = high.shape[0]
    nodes = latent.shape[0]
    groups = blocks // BLOCKS_PER_GROUP
    group_nodes = nodes // groups
    group_slots = BLOCKS_PER_GROUP * LANES
    table_rows, width = table_ref.shape
    per_slab = table_rows // LANES
    recv = jnp.concatenate([dot(latent, lr_own[...]), dot(latent, lr_oth[...])], axis=1)
    recv_high = recv.astype(BF16).astype(F32)
    recv_low = recv - recv_high
    edge = jnp.concatenate([le_own[...], le_oth[...]], axis=1).astype(F32)
    base = (kind * per_slab + 1).astype(F32)
    local = high - base
    valid = (local >= 0.0) & (local < float(per_slab))
    flag = jnp.where(valid, 1.0, 0.0)
    flag16 = flag.astype(BF16)
    inclusive = dot(flag16, ones_where(iota((LANES, LANES), 0) <= iota((LANES, LANES), 1)))
    square = (blocks, blocks)
    ahead = ones_where(
        (iota(square, 1) < iota(square, 0))
        & (iota(square, 1) // BLOCKS_PER_GROUP == iota(square, 0) // BLOCKS_PER_GROUP)
    )
    offset = jnp.sum(dot(ahead, flag16), axis=1, keepdims=True)
    rank = jnp.where(valid, inclusive - flag + offset, -1.0)
    ranks[...] = rank
    node_rows = jnp.where(
        iota((group_nodes, group_slots), 1) // slots == iota((group_nodes, group_slots), 0), 1.0, 0.0
    )

    def pooled(rank_rows, start, columns, terms):
        wanted = iota((CHUNK, LANES), 0).astype(F32) + start
        select = jnp.concatenate([ones_where(r == wanted) for r in rank_rows], axis=1)
        compact = dot_on(select, columns, 1, 1)
        row = (compact[:, 4:5] * float(LANES) + compact[:, 5:6]).astype(jnp.int32)
        choose = ones_where(row == iota((CHUNK, table_rows), 1))
        compact = compact.astype(BF16)
        pre = dot(choose, table_ref[...]) + dot(compact, terms)
        return dot_on(compact[:, 8 : 8 + group_nodes], silu(pre).astype(BF16), 0, 0)

    for g in range(groups):
        at = g * BLOCKS_PER_GROUP
        n0 = g * group_nodes
        line = lambda a: jnp.concatenate(
            [a[at + k : at + k + 1, :] for k in range(BLOCKS_PER_GROUP)], axis=1
        )
        columns = jnp.concatenate(
            [
                feats[g],
                line(local),
                line(low),
                jnp.zeros((2, group_slots), F32),
                node_rows,
                node_rows,
                jnp.zeros((8, group_slots), F32),
            ],
            axis=0,
        ).astype(BF16)
        terms = jnp.concatenate(
            [
                edge,
                jnp.zeros((4, width), F32),
                recv_high[n0 : n0 + group_nodes],
                recv_low[n0 : n0 + group_nodes],
                jnp.zeros((8, width), F32),
            ],
            axis=0,
        ).astype(BF16)
        payload[g] = columns
        right[g] = terms
        rows = [rank[at + k : at + k + 1, :] for k in range(BLOCKS_PER_GROUP)]
        out_ref[n0 : n0 + group_nodes, :] = pooled(rows, 0.0, columns, terms)
    for g in range(groups):
        at = g * BLOCKS_PER_GROUP
        n0 = g * group_nodes
        count = jnp.sum(flag[at : at + BLOCKS_PER_GROUP]).astype(jnp.int32)

        @pl.loop(1, (count + CHUNK - 1) // CHUNK)
        def _(step):
            rows = [ranks[at + k : at + k + 1, :] for k in range(BLOCKS_PER_GROUP)]
            out_ref[n0 : n0 + group_nodes, :] += pooled(
                rows, (step * CHUNK).astype(F32), payload[g], right[g]
            )


def unpack(packed_ref, nodes, slots):
    width = packed_ref.shape[1]
    blocks = nodes * slots // LANES
    tail = packed_ref[nodes:, :].astype(F32)
    feat_rows = tail.shape[0] - blocks
    high = tail[feat_rows:, 0:LANES]
    low = tail[feat_rows:, LANES : 2 * LANES]
    per_group = BLOCKS_PER_GROUP * LANES // width
    feats = []
    for g in range(blocks // BLOCKS_PER_GROUP):
        rows = [tail[4 * k : 4 * k + 4] for k in range(g * per_group, (g + 1) * per_group)]
        feats.append(jnp.concatenate(rows, axis=1))
    return high, low, feats


def own_pool_body(nodes, slots, packed_ref, table_ref, lr_own, lr_oth, le_own, le_oth, out_ref, payload, ranks, right):
    first = lax.axis_index("ch") == 0
    high, low, feats = unpack(packed_ref, nodes, slots)
    half_blocks = high.shape[0] // 2
    half_groups = len(feats) // 2
    pick = lambda a, b: jnp.where(first, a, b)
    latent = pick(packed_ref[0 : nodes // 2, :], packed_ref[nodes // 2 : nodes, :])
    pool_part(
        pick(high[:half_blocks], high[half_blocks:]),
        pick(low[:half_blocks], low[half_blocks:]),
        [pick(feats[k], feats[half_groups + k]) for k in range(half_groups)],
        latent,
        jnp.int32(1),
        slots,
        table_ref,
        (lr_own, lr_oth, le_own, le_oth),
        payload,
        ranks,
        right,
        out_ref,
    )


def near_pool_body(nodes, slots, packed_ref, table_ref, lr_own, lr_oth, le_own, le_oth, out_ref, payload, ranks, right, total):
    high, low, feats = unpack(packed_ref, nodes, slots)
    kind = 2 * lax.axis_index("ch")
    pool_part(
        high,
        low,
        feats,
        packed_ref[0:nodes, :],
        kind,
        slots,
        table_ref,
        (lr_own, lr_oth, le_own, le_oth),
        payload,
        ranks,
        right,
        total,
    )
    out_ref[...] = total[...].astype(BF16)


def middle_body(packed_ref, near_ref, near_oth_ref, own_ref, own_oth_ref, lo_own, lo_oth, ps, pr, mid_ref, send_ref, recv_ref):
    first = lax.axis_index("ch") == 0
    half = lo_own.shape[0]
    nodes = near_ref.shape[0]
    mine, theirs = own_ref[...], own_oth_ref[...]
    flip = lambda a: jnp.concatenate([a[:, half:], a[:, :half]], axis=1)
    theirs = flip(theirs)
    total = near_ref[...].astype(F32) + flip(near_oth_ref[...]).astype(F32)
    total = total + jnp.concatenate(
        [jnp.where(first, mine, theirs), jnp.where(first, theirs, mine)], axis=0
    )
    pool = total.astype(BF16)
    agg = dot(pool[:, :half], lo_own[...]) + dot(pool[:, half:], lo_oth[...])
    mid = (packed_ref[0:nodes, :].astype(F32) + agg).astype(BF16)
    mid_ref[...] = mid
    send_ref[...] = dot(mid, ps[...]).astype(BF16)
    recv_ref[...] = dot(mid, pr[...])


def edge_body(patches, piece_ref, recv_ref, senders_ref, receivers_ref, limit_ref, feats_ref, pe, pool_ref):
    nodes = recv_ref.shape[0]
    rows = patches * nodes
    slots = senders_ref.shape[1] * rows // piece_ref.shape[0]
    recv = recv_ref[...]
    recv_high = recv.astype(BF16)
    recv_low = (recv - recv_high.astype(F32)).astype(BF16)
    total = None
    for k in range(piece_ref.shape[0] // rows):
        lanes = slice(k * slots, (k + 1) * slots)
        patch = iota((1, slots), 1) // (slots // patches)
        choose = ones_where(iota((rows, slots), 0) == senders_ref[:, lanes] + patch * nodes)
        into = iota((nodes, slots), 0) == receivers_ref[:, lanes]
        into16 = ones_where(into)
        pre = (
            dot_on(choose, piece_ref[k * rows : (k + 1) * rows, :], 0, 0)
            + dot_on(into16, recv_high, 0, 0)
            + dot_on(into16, recv_low, 0, 0)
            + dot_on(feats_ref[:, lanes], pe[...], 0, 0)
        )
        act = silu(pre).astype(BF16)
        part = dot(ones_where(into & (limit_ref[:, lanes] > 0)), act)
        total = part if total is None else total + part
    pool_ref[...] = total.astype(BF16)


def node_body(mid_ref, pool_ref, pool_oth_ref, po_own, po_oth, nf_own, nf_oth, ns_own, ns_oth, gain_ref, out_ref):
    first = lax.axis_index("ch") == 0
    width = mid_ref.shape[1]
    half = width // 2
    mid = mid_ref[...]
    agg = (dot(pool_ref[...], po_own[...]) + dot(pool_oth_ref[...], po_oth[...])).astype(BF16)
    update = None
    for nf, ns in ((nf_own, ns_own), (nf_oth, ns_oth)):
        hidden = silu(dot(mid, nf[0:width, :]) + dot(agg, nf[width:, :])).astype(BF16)
        term = dot(hidden, ns[...])
        update = term if update is None else update + term
    mean = jnp.sum(update, axis=1, keepdims=True) / width
    square = jnp.sum(update * update, axis=1, keepdims=True) / width
    scale = lax.rsqrt(square - mean * mean + 1e-05)
    pick = lambda a: jnp.where(first, a[:, :half], a[:, half:])
    out_ref[...] = (
        pick(mid).astype(F32) + (pick(update) - mean) * scale * gain_ref[...]
    ).astype(BF16)


def per_device(
    grid_input,
    grid_senders,
    grid_lengths,
    grid_feats,
    mesh_latent,
    mesh_senders,
    mesh_receivers,
    mesh_counts,
    mesh_feats,
    embed_first,
    embed_second,
    link_sender,
    link_receiver,
    link_edge,
    link_out,
    proc_sender,
    proc_receiver,
    proc_edge,
    proc_out,
    node_first,
    node_second,
    norm_gain,
):
    bands = lax.axis_size("band")
    slab_rows = grid_input.shape[0]
    nodes, slots = grid_senders.shape
    half = link_sender.shape[1]
    width = 2 * half
    capacity = mesh_senders.shape[1]
    edges = bands * capacity
    other = lambda a: lax.ppermute(a, "ch", [(0, 1), (1, 0)])
    at = lambda b, c: 2 * b + c
    to_owner = [(at(b + 1, 0), at(b, 0)) for b in range(bands - 1)]
    to_owner += [(at(b, 1), at(b + 1, 1)) for b in range(bands - 1)]
    to_patch = [(d, s) for s, d in to_owner]
    shape = jax.ShapeDtypeStruct

    latent_other = other(mesh_latent)
    packed_rows = nodes + 4 * (nodes * slots // width) + nodes * slots // LANES
    packed = call(
        functools.partial(pack_body, slab_rows),
        shape((packed_rows, width), BF16),
        (grid_senders.T, grid_lengths.reshape(1, nodes), grid_feats, mesh_latent, latent_other),
        scratch=[pltpu.VMEM((nodes, slots), F32)],
    )
    near_packed = lax.ppermute(packed, ("band", "ch"), to_owner)

    tile = slab_rows // 4
    fixed = lambda a: pl.BlockSpec(a.shape, lambda i: (0, 0))
    embed_weights = []
    for w in (embed_first, embed_second, link_sender):
        embed_weights += [w, other(w)]
    table = call(
        embed_body,
        shape((slab_rows, width), BF16),
        (grid_input.T, *embed_weights),
        grid=(slab_rows // tile,),
        in_specs=[pl.BlockSpec((grid_input.shape[1], tile), lambda i: (0, i))]
        + [fixed(w) for w in embed_weights],
        out_specs=pl.BlockSpec((tile, width), lambda i: (i, 0)),
        flops=2 * slab_rows * width * (256 + 2 * width),
        moved=4 * 1024 * 1024,
    )

    link_weights = (link_receiver, other(link_receiver), link_edge, other(link_edge))
    group_slots = BLOCKS_PER_GROUP * LANES
    group_nodes = group_slots // slots
    blocks = nodes * slots // LANES
    scratch = lambda count: [
        pltpu.VMEM((count // BLOCKS_PER_GROUP, 16 + 2 * group_nodes, group_slots), BF16),
        pltpu.VMEM((count, LANES), F32),
        pltpu.VMEM((count // BLOCKS_PER_GROUP, 16 + 2 * group_nodes, width), BF16),
    ]
    own = call(
        functools.partial(own_pool_body, nodes, slots),
        shape((nodes // 2, width), F32),
        (packed, table, *link_weights),
        scratch=scratch(blocks // 2),
        flops=4 * 10**9,
        moved=4 * 1024 * 1024,
    )
    own_other = other(own)
    near = call(
        functools.partial(near_pool_body, nodes, slots),
        shape((nodes, width), BF16),
        (near_packed, table, *link_weights),
        scratch=scratch(blocks) + [pltpu.VMEM((nodes, width), F32)],
        flops=4 * 10**9,
        moved=4 * 1024 * 1024,
    )
    near_back = lax.ppermute(near, ("band", "ch"), to_patch)
    near_back_other = other(near_back)

    mid, send, recv = call(
        middle_body,
        (shape((nodes, width), BF16), shape((nodes, half), BF16), shape((nodes, half), F32)),
        (packed, near_back, near_back_other, own, own_other, link_out, other(link_out), proc_sender, proc_receiver),
    )
    spread = jnp.broadcast_to(send[None], (bands, nodes, half)).reshape(bands * nodes, half)
    piece = lax.all_to_all(spread, "band", 0, 0, tiled=True)

    limit = (
        mesh_counts.reshape(bands, 1) - jnp.arange(capacity, dtype=jnp.int32)[None, :]
    ).reshape(1, edges)
    pool = call(
        functools.partial(edge_body, LANES // capacity),
        shape((nodes, half), BF16),
        (piece, recv, mesh_senders.reshape(1, edges), mesh_receivers.reshape(1, edges), limit, mesh_feats, proc_edge),
    )
    return call(
        node_body,
        shape((nodes, half), BF16),
        (
            mid,
            pool,
            other(pool),
            proc_out,
            other(proc_out),
            node_first,
            other(node_first),
            node_second,
            other(node_second),
            norm_gain.reshape(1, half),
        ),
    )


def solution(mesh):
    rows = P(("grp", "band"), None)
    columns = P(None, ("grp", "band"))
    split = P(("grp", "band"), "ch")
    by_column = P(None, "ch")
    by_row = P("ch", None)
    in_specs = (
        rows,
        rows,
        P(("grp", "band")),
        columns,
        split,
        rows,
        rows,
        rows,
        columns,
        by_column,
        by_row,
        by_column,
        by_column,
        by_column,
        by_row,
        by_column,
        by_column,
        by_column,
        by_row,
        by_column,
        by_row,
        P("ch"),
    )
    return jax.shard_map(
        per_device, mesh=mesh, in_specs=in_specs, out_specs=split, check_vma=False
    )
```

```python
import functools

import jax
import jax.numpy as jnp
from jax import lax
from jax.experimental import pallas as pl
from jax.experimental.pallas import tpu as pltpu
from jax.sharding import PartitionSpec as P

F32 = jnp.float32
BF16 = jnp.bfloat16
LANES = 128
CHUNK = 256
PAYLOAD_ROWS = 16
BLOCKS_PER_GROUP = 8
VMEM_LIMIT = 48 * 1024 * 1024


def dot(a, b):
    return jnp.dot(a, b, preferred_element_type=F32)


def dot_on(a, b, dim_a, dim_b):
    return lax.dot_general(a, b, (((dim_a,), (dim_b,)), ((), ())), preferred_element_type=F32)


def silu(v):
    return 0.5 * v * (1.0 + jnp.tanh(0.5 * v))


def iota(shape, dim):
    return lax.broadcasted_iota(jnp.int32, shape, dim)


def ones_where(mask):
    return jnp.where(mask, 1.0, 0.0).astype(BF16)


def call(body, out_shape, args, grid_spec=None, flops=0, moved=0, scratch=(), **kw):
    whole = pl.BlockSpec(memory_space=pltpu.VMEM)
    if "in_specs" not in kw:
        kw["in_specs"] = [whole] * len(args)
        kw["out_specs"] = jax.tree.map(lambda _: whole, out_shape)
    return pl.pallas_call(
        body,
        out_shape=out_shape,
        scratch_shapes=list(scratch),
        compiler_params=pltpu.CompilerParams(vmem_limit_bytes=VMEM_LIMIT),
        cost_estimate=pl.CostEstimate(flops=flops, bytes_accessed=moved, transcendentals=0),
        **kw,
    )(*args)


def pack_body(slab_rows, senders_hbm, lengths_hbm, feats_hbm, own_hbm, other_ref, out_ref, senders_ref, lengths_ref, feats_ref, own_ref, turned, sems):
    copies = fetch(
        [(senders_hbm, senders_ref), (lengths_hbm, lengths_ref), (feats_hbm, feats_ref), (own_hbm, own_ref)],
        sems,
    )
    for c in copies:
        c.wait()
    band = lax.axis_index("band")
    core = lax.axis_index("ch")
    slots, nodes = senders_ref.shape
    width = out_ref.shape[1]
    turned[...] = (senders_ref[...] - (band - 1) * slab_rows).astype(F32).T
    own, other = own_ref[...], other_ref[...]
    first = core == 0
    out_ref[0:nodes, :] = jnp.concatenate(
        [jnp.where(first, own, other), jnp.where(first, other, own)], axis=1
    )
    per_row = LANES // slots
    rows = nodes // per_row
    pieces = [turned[pl.ds(j, rows, stride=per_row), :] for j in range(per_row)]
    index = jnp.concatenate(pieces, axis=1).astype(jnp.int32)
    shape = (rows, LANES)
    spread = jnp.where(
        iota((rows, nodes), 1) // per_row == iota((rows, nodes), 0),
        lengths_ref[...].astype(F32),
        0.0,
    ).astype(BF16)
    pick = ones_where(iota((nodes, LANES), 0) % per_row == iota((nodes, LANES), 1) // slots)
    length = dot(spread, pick)
    used = (iota(shape, 1) % slots).astype(F32) < length
    high = jnp.where(used, index // LANES + 1, 0).astype(F32)
    low = jnp.where(used, index % LANES, 0).astype(F32)
    fill = jnp.zeros((rows, width - 2 * LANES), F32)
    feats = feats_ref[...].astype(F32)
    parts = [feats[:, k * width : (k + 1) * width] for k in range(feats.shape[1] // width)]
    tail = jnp.concatenate(parts + [jnp.concatenate([high, low, fill], axis=1)], axis=0)
    out_ref[nodes:, :] = tail.astype(BF16)


def fetch(moves, sems):
    copies = [pltpu.make_async_copy(src, dst, sems.at[k]) for k, (src, dst) in enumerate(moves)]
    for c in copies:
        c.start()
    return copies


def embed_body(tile, x_hbm, f_hbm, s_hbm, l_hbm, f_oth, s_oth, l_oth, out_ref, x_ref, f_own, s_own, l_own, first_t, second_t, third_t, sems):
    half = f_oth.shape[1]
    tiles = x_ref.shape[1] // tile
    moves = [(f_hbm, f_own), (s_hbm, s_own), (l_hbm, l_own)]
    moves += [
        (x_hbm.at[:, pl.ds(k * tile, tile)], x_ref.at[:, pl.ds(k * tile, tile)]) for k in range(tiles)
    ]
    copies = fetch(moves, sems)
    first_t[half:, :] = f_oth[...].T
    second_t[:, half:] = s_oth[...].T
    third_t[half:, :] = l_oth[...].T
    for c in copies[:3]:
        c.wait()
    first_t[:half, :] = f_own[...].T
    second_t[:, :half] = s_own[...].T
    third_t[:half, :] = l_own[...].T
    for c in copies[3:]:
        c.wait()

    @pl.loop(0, tiles)
    def _(k):
        at = pl.ds(pl.multiple_of(k * tile, tile), tile)
        hidden = silu(dot(first_t[...], x_ref[:, at])).astype(BF16)
        latent = dot(second_t[...], hidden).astype(BF16)
        out_ref[:, at] = dot(third_t[...], latent).astype(BF16)


def running(flag16, together):
    blocks = flag16.shape[0]
    inclusive = dot(flag16, ones_where(iota((LANES, LANES), 0) <= iota((LANES, LANES), 1)))
    square = (blocks, blocks)
    earlier = iota(square, 1) < iota(square, 0)
    earlier &= iota(square, 1) // together == iota(square, 0) // together
    return inclusive + jnp.sum(dot(ones_where(earlier), flag16), axis=1, keepdims=True)


def pool_part(high, low, feats, latent, kind, slots, table_ref, weights, payload, late, right, out_ref):
    lr_own, lr_oth, le_own, le_oth = weights
    blocks = high.shape[0]
    nodes = latent.shape[0]
    groups = blocks // BLOCKS_PER_GROUP
    group_nodes = nodes // groups
    group_slots = BLOCKS_PER_GROUP * LANES
    width, table_rows = table_ref.shape
    per_slab = table_rows // LANES
    recv = jnp.concatenate([dot(latent, lr_own[...]), dot(latent, lr_oth[...])], axis=1)
    edge = jnp.concatenate([le_own[...], le_oth[...]], axis=1).astype(F32)
    right[0:nodes, :] = recv.astype(BF16)
    right[nodes:, :] = jnp.concatenate(
        [edge, jnp.zeros((PAYLOAD_ROWS - edge.shape[0], width), F32)], axis=0
    ).astype(BF16)
    base = (kind * per_slab + 1).astype(F32)
    local = high - base
    valid = (local >= 0.0) & (local < float(per_slab))
    flag = jnp.where(valid, 1.0, 0.0)
    rank = running(flag.astype(BF16), BLOCKS_PER_GROUP) - 1.0
    over = valid & (rank >= float(CHUNK))
    over_flag = jnp.where(over, 1.0, 0.0)
    late[...] = jnp.where(over, running(over_flag.astype(BF16), blocks) - 1.0, -1.0)
    rank = jnp.where(valid, rank, -1.0)
    spot = iota((1, group_slots), 1) // slots
    place = iota((CHUNK, LANES), 0).astype(F32)

    def picked(rows, start, columns):
        select = jnp.concatenate([ones_where(r == place + start) for r in rows], axis=1)
        return dot_on(columns, select, 1, 1)

    def pooled(compact):
        count = compact.shape[1]
        own_node = ones_where(iota((nodes, count), 0).astype(F32) + 1.0 == compact[6:7, :])
        one_low = ones_where(iota((LANES, count), 0).astype(F32) == compact[5:6, :])
        row_high = compact[4:5, :]
        choose = jnp.concatenate(
            [one_low * ones_where(row_high == float(k)) for k in range(per_slab)], axis=0
        )
        terms = jnp.concatenate([own_node, compact.astype(BF16)], axis=0)
        pre = dot(table_ref[...], choose) + dot_on(right[...], terms, 0, 0)
        return dot_on(silu(pre).astype(BF16), own_node, 1, 1)

    parts = []
    for g in range(groups):
        at = g * BLOCKS_PER_GROUP
        line = lambda a: jnp.concatenate(
            [a[at + k : at + k + 1, :] for k in range(BLOCKS_PER_GROUP)], axis=1
        )
        columns = jnp.concatenate(
            [
                feats[g],
                line(local),
                line(low),
                (spot + g * group_nodes + 1).astype(F32),
                jnp.zeros((PAYLOAD_ROWS - 7, group_slots), F32),
            ],
            axis=0,
        ).astype(BF16)
        payload[g] = columns
        rows = [rank[at + k : at + k + 1, :] for k in range(BLOCKS_PER_GROUP)]
        parts.append(picked(rows, 0.0, columns))
    out_ref[...] = pooled(jnp.concatenate(parts, axis=1))
    count = jnp.sum(over_flag).astype(jnp.int32)

    @pl.loop(0, (count + CHUNK - 1) // CHUNK)
    def _(step):
        start = (step * CHUNK).astype(F32)
        total = None
        for g in range(groups):
            at = g * BLOCKS_PER_GROUP
            rows = [late[at + k : at + k + 1, :] for k in range(BLOCKS_PER_GROUP)]
            term = picked(rows, start, payload[g])
            total = term if total is None else total + term
        out_ref[...] += pooled(total)


def unpack(packed_ref, nodes, slots):
    width = packed_ref.shape[1]
    blocks = nodes * slots // LANES
    tail = packed_ref[nodes:, :].astype(F32)
    feat_rows = tail.shape[0] - blocks
    high = tail[feat_rows:, 0:LANES]
    low = tail[feat_rows:, LANES : 2 * LANES]
    per_group = BLOCKS_PER_GROUP * LANES // width
    feats = []
    for g in range(blocks // BLOCKS_PER_GROUP):
        rows = [tail[4 * k : 4 * k + 4] for k in range(g * per_group, (g + 1) * per_group)]
        feats.append(jnp.concatenate(rows, axis=1))
    return high, low, feats


def own_pool_body(nodes, slots, packed_ref, table_ref, lr_own, lr_oth, le_own, le_oth, out_ref, payload, late, right):
    first = lax.axis_index("ch") == 0
    high, low, feats = unpack(packed_ref, nodes, slots)
    half_blocks = high.shape[0] // 2
    half_groups = len(feats) // 2
    pick = lambda a, b: jnp.where(first, a, b)
    latent = pick(packed_ref[0 : nodes // 2, :], packed_ref[nodes // 2 : nodes, :])
    pool_part(
        pick(high[:half_blocks], high[half_blocks:]),
        pick(low[:half_blocks], low[half_blocks:]),
        [pick(feats[k], feats[half_groups + k]) for k in range(half_groups)],
        latent,
        jnp.int32(1),
        slots,
        table_ref,
        (lr_own, lr_oth, le_own, le_oth),
        payload,
        late,
        right,
        out_ref,
    )


def near_pool_body(nodes, slots, packed_ref, table_ref, lr_own, lr_oth, le_own, le_oth, out_ref, payload, late, right, total):
    high, low, feats = unpack(packed_ref, nodes, slots)
    kind = 2 * lax.axis_index("ch")
    pool_part(
        high,
        low,
        feats,
        packed_ref[0:nodes, :],
        kind,
        slots,
        table_ref,
        (lr_own, lr_oth, le_own, le_oth),
        payload,
        late,
        right,
        total,
    )
    out_ref[...] = total[...].astype(BF16)


def middle_body(packed_ref, near_ref, near_oth_ref, own_ref, own_oth_ref, lo_own, lo_oth, ps, pr, mid_ref, send_ref, recv_ref):
    first = lax.axis_index("ch") == 0
    half = lo_own.shape[0]
    nodes = near_ref.shape[1]
    mine, theirs = own_ref[...], own_oth_ref[...]
    flip = lambda a: jnp.concatenate([a[half:, :], a[:half, :]], axis=0)
    theirs = flip(theirs)
    total = near_ref[...].astype(F32) + flip(near_oth_ref[...]).astype(F32)
    total = total + jnp.concatenate(
        [jnp.where(first, mine, theirs), jnp.where(first, theirs, mine)], axis=1
    )
    pool = total.astype(BF16).T
    agg = dot(pool[:, :half], lo_own[...]) + dot(pool[:, half:], lo_oth[...])
    mid = (packed_ref[0:nodes, :].astype(F32) + agg).astype(BF16)
    mid_ref[...] = mid
    send_ref[...] = dot(mid, ps[...]).astype(BF16)
    recv_ref[...] = dot(mid, pr[...])


def edge_body(patches, piece_ref, recv_ref, senders_ref, receivers_ref, limit_ref, feats_ref, pe, pool_ref):
    nodes = recv_ref.shape[0]
    rows = patches * nodes
    slots = senders_ref.shape[1] * rows // piece_ref.shape[0]
    recv = recv_ref[...]
    recv_high = recv.astype(BF16)
    recv_low = (recv - recv_high.astype(F32)).astype(BF16)
    total = None
    for k in range(piece_ref.shape[0] // rows):
        lanes = slice(k * slots, (k + 1) * slots)
        patch = iota((1, slots), 1) // (slots // patches)
        choose = ones_where(iota((rows, slots), 0) == senders_ref[:, lanes] + patch * nodes)
        into = iota((nodes, slots), 0) == receivers_ref[:, lanes]
        into16 = ones_where(into)
        pre = (
            dot_on(choose, piece_ref[k * rows : (k + 1) * rows, :], 0, 0)
            + dot_on(into16, recv_high, 0, 0)
            + dot_on(into16, recv_low, 0, 0)
            + dot_on(feats_ref[:, lanes], pe[...], 0, 0)
        )
        act = silu(pre).astype(BF16)
        part = dot(ones_where(into & (limit_ref[:, lanes] > 0)), act)
        total = part if total is None else total + part
    pool_ref[...] = total.astype(BF16)


def node_body(mid_ref, pool_ref, pool_oth_ref, po_own, po_oth, nf_own, nf_oth, ns_own, ns_oth, gain_ref, out_ref):
    first = lax.axis_index("ch") == 0
    width = mid_ref.shape[1]
    half = width // 2
    mid = mid_ref[...]
    agg = (dot(pool_ref[...], po_own[...]) + dot(pool_oth_ref[...], po_oth[...])).astype(BF16)
    update = None
    for nf, ns in ((nf_own, ns_own), (nf_oth, ns_oth)):
        hidden = silu(dot(mid, nf[0:width, :]) + dot(agg, nf[width:, :])).astype(BF16)
        term = dot(hidden, ns[...])
        update = term if update is None else update + term
    mean = jnp.sum(update, axis=1, keepdims=True) / width
    square = jnp.sum(update * update, axis=1, keepdims=True) / width
    scale = lax.rsqrt(square - mean * mean + 1e-05)
    pick = lambda a: jnp.where(first, a[:, :half], a[:, half:])
    out_ref[...] = (
        pick(mid).astype(F32) + (pick(update) - mean) * scale * gain_ref[...]
    ).astype(BF16)


def per_device(
    grid_input,
    grid_senders,
    grid_lengths,
    grid_feats,
    mesh_latent,
    mesh_senders,
    mesh_receivers,
    mesh_counts,
    mesh_feats,
    embed_first,
    embed_second,
    link_sender,
    link_receiver,
    link_edge,
    link_out,
    proc_sender,
    proc_receiver,
    proc_edge,
    proc_out,
    node_first,
    node_second,
    norm_gain,
):
    bands = lax.axis_size("band")
    slab_rows = grid_input.shape[0]
    nodes, slots = grid_senders.shape
    half = link_sender.shape[1]
    width = 2 * half
    capacity = mesh_senders.shape[1]
    edges = bands * capacity
    other = lambda a: lax.ppermute(a, "ch", [(0, 1), (1, 0)])
    at = lambda b, c: 2 * b + c
    to_owner = [(at(b + 1, 0), at(b, 0)) for b in range(bands - 1)]
    to_owner += [(at(b, 1), at(b + 1, 1)) for b in range(bands - 1)]
    to_patch = [(d, s) for s, d in to_owner]
    shape = jax.ShapeDtypeStruct

    hbm = pl.BlockSpec(memory_space=pltpu.HBM)
    vmem = pl.BlockSpec(memory_space=pltpu.VMEM)
    latent_other = other(mesh_latent)
    packed_rows = nodes + 4 * (nodes * slots // width) + nodes * slots // LANES
    pack_inputs = (grid_senders.T, grid_lengths.reshape(1, nodes), grid_feats, mesh_latent)
    packed = call(
        functools.partial(pack_body, slab_rows),
        shape((packed_rows, width), BF16),
        (*pack_inputs, latent_other),
        in_specs=[hbm] * 4 + [vmem],
        out_specs=vmem,
        scratch=[pltpu.VMEM(a.shape, a.dtype) for a in pack_inputs]
        + [pltpu.VMEM((nodes, slots), F32), pltpu.SemaphoreType.DMA((4,))],
    )
    near_packed = lax.ppermute(packed, ("band", "ch"), to_owner)

    tile = slab_rows // 4
    embed_weights = (embed_first, embed_second, link_sender)
    inputs = grid_input.shape[1]
    table = call(
        functools.partial(embed_body, tile),
        shape((width, slab_rows), BF16),
        (grid_input.T, *embed_weights, *[other(w) for w in embed_weights]),
        in_specs=[hbm] * 4 + [vmem] * 3,
        out_specs=vmem,
        scratch=[pltpu.VMEM((inputs, slab_rows), BF16)]
        + [pltpu.VMEM(w.shape, BF16) for w in embed_weights]
        + [pltpu.VMEM((width, n), BF16) for n in (inputs, width, width)]
        + [pltpu.SemaphoreType.DMA((3 + slab_rows // tile,))],
        flops=2 * slab_rows * width * (256 + 2 * width),
        moved=4 * 1024 * 1024,
    )

    link_weights = (link_receiver, other(link_receiver), link_edge, other(link_edge))
    group_slots = BLOCKS_PER_GROUP * LANES
    blocks = nodes * slots // LANES
    scratch = lambda count: [
        pltpu.VMEM((count // BLOCKS_PER_GROUP, PAYLOAD_ROWS, group_slots), BF16),
        pltpu.VMEM((count, LANES), F32),
        pltpu.VMEM((PAYLOAD_ROWS + count * LANES // slots, width), BF16),
    ]
    own = call(
        functools.partial(own_pool_body, nodes, slots),
        shape((width, nodes // 2), F32),
        (packed, table, *link_weights),
        scratch=scratch(blocks // 2),
        flops=4 * 10**9,
        moved=4 * 1024 * 1024,
    )
    own_other = other(own)
    near = call(
        functools.partial(near_pool_body, nodes, slots),
        shape((width, nodes), BF16),
        (near_packed, table, *link_weights),
        scratch=scratch(blocks) + [pltpu.VMEM((width, nodes), F32)],
        flops=4 * 10**9,
        moved=4 * 1024 * 1024,
    )
    near_back = lax.ppermute(near, ("band", "ch"), to_patch)
    near_back_other = other(near_back)

    mid, send, recv = call(
        middle_body,
        (shape((nodes, width), BF16), shape((nodes, half), BF16), shape((nodes, half), F32)),
        (packed, near_back, near_back_other, own, own_other, link_out, other(link_out), proc_sender, proc_receiver),
    )
    spread = jnp.broadcast_to(send[None], (bands, nodes, half)).reshape(bands * nodes, half)
    piece = lax.all_to_all(spread, "band", 0, 0, tiled=True)

    limit = (
        mesh_counts.reshape(bands, 1) - jnp.arange(capacity, dtype=jnp.int32)[None, :]
    ).reshape(1, edges)
    pool = call(
        functools.partial(edge_body, LANES // capacity),
        shape((nodes, half), BF16),
        (piece, recv, mesh_senders.reshape(1, edges), mesh_receivers.reshape(1, edges), limit, mesh_feats, proc_edge),
    )
    return call(
        node_body,
        shape((nodes, half), BF16),
        (
            mid,
            pool,
            other(pool),
            proc_out,
            other(proc_out),
            node_first,
            other(node_first),
            node_second,
            other(node_second),
            norm_gain.reshape(1, half),
        ),
    )


def solution(mesh):
    rows = P(("grp", "band"), None)
    columns = P(None, ("grp", "band"))
    split = P(("grp", "band"), "ch")
    by_column = P(None, "ch")
    by_row = P("ch", None)
    in_specs = (
        rows,
        rows,
        P(("grp", "band")),
        columns,
        split,
        rows,
        rows,
        rows,
        columns,
        by_column,
        by_row,
        by_column,
        by_column,
        by_column,
        by_row,
        by_column,
        by_column,
        by_column,
        by_row,
        by_column,
        by_row,
        P("ch"),
    )
    return jax.shard_map(
        per_device, mesh=mesh, in_specs=in_specs, out_specs=split, check_vma=False
    )
```

```python
import functools

import jax
import jax.numpy as jnp
from jax import lax
from jax.experimental import pallas as pl
from jax.experimental.pallas import tpu as pltpu
from jax.sharding import PartitionSpec as P

F32 = jnp.float32
BF16 = jnp.bfloat16
LANES = 128
CHUNK = 256
SPARE = 128
PAYLOAD_ROWS = 16
BLOCKS_PER_GROUP = 8
VMEM_LIMIT = 48 * 1024 * 1024


def dot(a, b):
    return jnp.dot(a, b, preferred_element_type=F32)


def dot_on(a, b, dim_a, dim_b):
    return lax.dot_general(a, b, (((dim_a,), (dim_b,)), ((), ())), preferred_element_type=F32)


def silu(v):
    return 0.5 * v * (1.0 + jnp.tanh(0.5 * v))


def iota(shape, dim):
    return lax.broadcasted_iota(jnp.int32, shape, dim)


def ones_where(mask):
    return jnp.where(mask, 1.0, 0.0).astype(BF16)


def call(body, out_shape, args, grid_spec=None, flops=0, moved=0, scratch=(), **kw):
    whole = pl.BlockSpec(memory_space=pltpu.VMEM)
    if "in_specs" not in kw:
        kw["in_specs"] = [whole] * len(args)
        kw["out_specs"] = jax.tree.map(lambda _: whole, out_shape)
    return pl.pallas_call(
        body,
        out_shape=out_shape,
        scratch_shapes=list(scratch),
        compiler_params=pltpu.CompilerParams(vmem_limit_bytes=VMEM_LIMIT),
        cost_estimate=pl.CostEstimate(flops=flops, bytes_accessed=moved, transcendentals=0),
        **kw,
    )(*args)


def tail_body(slab_rows, width, senders_hbm, lengths_hbm, feats_hbm, mesh_hbm, out_ref, request_ref, senders_ref, lengths_ref, feats_ref, mesh_ref, turned, sems):
    band = lax.axis_index("band")
    copies = fetch(
        [(senders_hbm, senders_ref), (lengths_hbm, lengths_ref), (feats_hbm, feats_ref), (mesh_hbm, mesh_ref)], sems
    )
    for c in copies:
        c.wait()
    slots, nodes = senders_ref.shape
    turned[...] = (senders_ref[...] - (band - 1) * slab_rows).astype(F32).T
    per_row = LANES // slots
    rows = nodes // per_row
    pieces = [turned[pl.ds(j, rows, stride=per_row), :] for j in range(per_row)]
    index = jnp.concatenate(pieces, axis=1).astype(jnp.int32)
    shape = (rows, LANES)
    spread = jnp.where(
        iota((rows, nodes), 1) // per_row == iota((rows, nodes), 0),
        lengths_ref[...].astype(F32),
        0.0,
    ).astype(BF16)
    pick = ones_where(iota((nodes, LANES), 0) % per_row == iota((nodes, LANES), 1) // slots)
    used = (iota(shape, 1) % slots).astype(F32) < dot(spread, pick)
    high = jnp.where(used, index // LANES + 1, 0).astype(F32)
    low = jnp.where(used, index % LANES, 0).astype(F32)
    half = rows // 2
    feats = feats_ref[...].astype(F32)
    parts = [feats[:, k * width : (k + 1) * width] for k in range(feats.shape[1] // width)]
    places = [high[:half], low[:half], high[half:], low[half:]]
    tail = jnp.concatenate(parts + [jnp.concatenate(places, axis=1)], axis=0)
    out_ref[...] = tail.astype(BF16)
    peers, capacity = mesh_ref.shape
    edges = peers * capacity
    peer = ones_where(iota((edges, peers), 0) // capacity == iota((edges, peers), 1))
    lists = dot(peer, mesh_ref[...].astype(F32).astype(BF16))
    own_slot = iota((edges, capacity), 0) % capacity == iota((edges, capacity), 1)
    single = jnp.where(own_slot, lists, 0.0).astype(BF16)
    request_ref[...] = dot(single, jnp.ones((capacity, width), BF16)).astype(BF16)


def pack_body(own_ref, other_ref, tail_ref, out_ref):
    first = lax.axis_index("ch") == 0
    nodes = own_ref.shape[0]
    own, other = own_ref[...], other_ref[...]
    out_ref[0:nodes, :] = jnp.concatenate(
        [jnp.where(first, own, other), jnp.where(first, other, own)], axis=1
    )
    out_ref[nodes:, :] = tail_ref[...]


def fetch(moves, sems):
    copies = [pltpu.make_async_copy(src, dst, sems.at[k]) for k, (src, dst) in enumerate(moves)]
    for c in copies:
        c.start()
    return copies


def embed_body(tile, x_hbm, f_hbm, s_hbm, l_hbm, f_oth, s_oth, l_oth, out_ref, x_ref, f_own, s_own, l_own, first_t, joint_t, sems):
    half = f_oth.shape[1]
    tiles = x_ref.shape[1] // tile
    moves = [(s_hbm, s_own), (l_hbm, l_own), (f_hbm, f_own)]
    moves += [
        (x_hbm.at[:, pl.ds(k * tile, tile)], x_ref.at[:, pl.ds(k * tile, tile)]) for k in range(tiles)
    ]
    copies = fetch(moves, sems)
    first_t[half:, :] = f_oth[...].T
    copies[0].wait()
    copies[1].wait()
    for k, s in ((0, s_own), (1, s_oth)):
        for j, l in ((0, l_own), (1, l_oth)):
            joint = dot(s[...], l[...]).astype(BF16)
            joint_t[j * half : (j + 1) * half, k * half : (k + 1) * half] = joint.T
    copies[2].wait()
    first_t[:half, :] = f_own[...].T
    for c in copies[3:]:
        c.wait()

    @pl.loop(0, tiles)
    def _(k):
        at = pl.ds(pl.multiple_of(k * tile, tile), tile)
        hidden = silu(dot(first_t[...], x_ref[:, at])).astype(BF16)
        out_ref[:, at] = dot(joint_t[...], hidden).astype(BF16)


def running(flag16, together):
    blocks = flag16.shape[0]
    inclusive = dot(flag16, ones_where(iota((LANES, LANES), 0) <= iota((LANES, LANES), 1)))
    square = (blocks, blocks)
    earlier = iota(square, 1) < iota(square, 0)
    earlier &= iota(square, 1) // together == iota(square, 0) // together
    return inclusive + jnp.sum(dot(ones_where(earlier), flag16), axis=1, keepdims=True)


def pool_part(high, low, feats, latent, kind, slots, room, spare, table_ref, weights, payload, late, right, out_ref):
    lr_own, lr_oth, le_own, le_oth = weights
    blocks = high.shape[0]
    nodes = latent.shape[0]
    groups = blocks // BLOCKS_PER_GROUP
    group_nodes = nodes // groups
    group_slots = BLOCKS_PER_GROUP * LANES
    width, table_rows = table_ref.shape
    per_slab = table_rows // LANES
    recv = jnp.concatenate([dot(latent, lr_own[...]), dot(latent, lr_oth[...])], axis=1)
    edge = jnp.concatenate([le_own[...], le_oth[...]], axis=1).astype(F32)
    right[0:nodes, :] = recv.astype(BF16)
    right[nodes:, :] = jnp.concatenate(
        [edge, jnp.zeros((PAYLOAD_ROWS - edge.shape[0], width), F32)], axis=0
    ).astype(BF16)
    base = (kind * per_slab + 1).astype(F32)
    local = high - base
    valid = (local >= 0.0) & (local < float(per_slab))
    flag = jnp.where(valid, 1.0, 0.0)
    rank = running(flag.astype(BF16), BLOCKS_PER_GROUP) - 1.0
    over = valid & (rank >= float(room))
    over_flag = jnp.where(over, 1.0, 0.0)
    late[...] = jnp.where(over, running(over_flag.astype(BF16), blocks) - 1.0, -1.0)
    rank = jnp.where(valid, rank, -1.0)
    spot = iota((1, group_slots), 1) // slots

    def picked(rows, start, count, columns):
        place = iota((count, LANES), 0).astype(F32) + start
        select = jnp.concatenate([ones_where(r == place) for r in rows], axis=1)
        return dot_on(columns, select, 1, 1)

    def picked_late(start, count):
        total = None
        for g in range(groups):
            at = g * BLOCKS_PER_GROUP
            rows = [late[at + k : at + k + 1, :] for k in range(BLOCKS_PER_GROUP)]
            term = picked(rows, start, count, payload[g])
            total = term if total is None else total + term
        return total

    def pooled(compact):
        count = compact.shape[1]
        own_node = ones_where(iota((nodes, count), 0).astype(F32) + 1.0 == compact[6:7, :])
        one_low = ones_where(iota((LANES, count), 0).astype(F32) == compact[5:6, :])
        row_high = compact[4:5, :]
        choose = jnp.concatenate(
            [one_low * ones_where(row_high == float(k)) for k in range(per_slab)], axis=0
        )
        terms = jnp.concatenate([own_node, compact.astype(BF16)], axis=0)
        pre = dot(table_ref[...], choose) + dot_on(right[...], terms, 0, 0)
        return dot_on(silu(pre).astype(BF16), own_node, 1, 1)

    parts = []
    for g in range(groups):
        at = g * BLOCKS_PER_GROUP
        line = lambda a: jnp.concatenate(
            [a[at + k : at + k + 1, :] for k in range(BLOCKS_PER_GROUP)], axis=1
        )
        columns = jnp.concatenate(
            [
                feats[g],
                line(local),
                line(low),
                (spot + g * group_nodes + 1).astype(F32),
                jnp.zeros((PAYLOAD_ROWS - 7, group_slots), F32),
            ],
            axis=0,
        ).astype(BF16)
        payload[g] = columns
        rows = [rank[at + k : at + k + 1, :] for k in range(BLOCKS_PER_GROUP)]
        parts.append(picked(rows, 0.0, room, columns))
    if spare:
        parts.append(picked_late(0.0, spare))
    out_ref[...] = pooled(jnp.concatenate(parts, axis=1))
    count = jnp.sum(over_flag).astype(jnp.int32)

    @pl.loop(0, jnp.maximum(count - spare + CHUNK - 1, 0) // CHUNK)
    def _(step):
        out_ref[...] += pooled(picked_late((step * CHUNK + spare).astype(F32), CHUNK))


def unpack(packed_ref, nodes, slots):
    width = packed_ref.shape[1]
    blocks = nodes * slots // LANES
    tail = packed_ref[nodes:, :].astype(F32)
    feat_rows = tail.shape[0] - blocks // 2
    place = lambda k: tail[feat_rows:, k * LANES : (k + 1) * LANES]
    high = jnp.concatenate([place(0), place(2)], axis=0)
    low = jnp.concatenate([place(1), place(3)], axis=0)
    per_group = BLOCKS_PER_GROUP * LANES // width
    feats = []
    for g in range(blocks // BLOCKS_PER_GROUP):
        rows = [tail[4 * k : 4 * k + 4] for k in range(g * per_group, (g + 1) * per_group)]
        feats.append(jnp.concatenate(rows, axis=1))
    return high, low, feats


def own_pool_body(nodes, slots, packed_ref, table_ref, lr_own, lr_oth, le_own, le_oth, out_ref, payload, late, right):
    first = lax.axis_index("ch") == 0
    high, low, feats = unpack(packed_ref, nodes, slots)
    half_blocks = high.shape[0] // 2
    half_groups = len(feats) // 2
    pick = lambda a, b: jnp.where(first, a, b)
    latent = pick(packed_ref[0 : nodes // 2, :], packed_ref[nodes // 2 : nodes, :])
    pool_part(
        pick(high[:half_blocks], high[half_blocks:]),
        pick(low[:half_blocks], low[half_blocks:]),
        [pick(feats[k], feats[half_groups + k]) for k in range(half_groups)],
        latent,
        jnp.int32(1),
        slots,
        2 * CHUNK,
        0,
        table_ref,
        (lr_own, lr_oth, le_own, le_oth),
        payload,
        late,
        right,
        out_ref,
    )


def near_pool_body(nodes, slots, packed_ref, table_ref, lr_own, lr_oth, le_own, le_oth, out_ref, payload, late, right, total):
    high, low, feats = unpack(packed_ref, nodes, slots)
    kind = 2 * lax.axis_index("ch")
    pool_part(
        high,
        low,
        feats,
        packed_ref[0:nodes, :],
        kind,
        slots,
        CHUNK,
        SPARE,
        table_ref,
        (lr_own, lr_oth, le_own, le_oth),
        payload,
        late,
        right,
        total,
    )
    out_ref[...] = total[...].astype(BF16)


def middle_body(packed_ref, near_ref, near_oth_ref, own_ref, own_oth_ref, lo_own, lo_oth, request_ref, mid_ref, rows_ref):
    first = lax.axis_index("ch") == 0
    half = lo_own.shape[0]
    nodes = near_ref.shape[1]
    mine, theirs = own_ref[...], own_oth_ref[...]
    flip = lambda a: jnp.concatenate([a[half:, :], a[:half, :]], axis=0)
    theirs = flip(theirs)
    total = near_ref[...].astype(F32) + flip(near_oth_ref[...]).astype(F32)
    total = total + jnp.concatenate(
        [jnp.where(first, mine, theirs), jnp.where(first, theirs, mine)], axis=1
    )
    pool = total.astype(BF16).T
    agg = dot(pool[:, :half], lo_own[...]) + dot(pool[:, half:], lo_oth[...])
    mid = (packed_ref[0:nodes, :].astype(F32) + agg).astype(BF16)
    mid_ref[...] = mid
    request = request_ref[...].astype(F32)
    wanted = ones_where(iota((request.shape[0], nodes), 1).astype(F32) == request[:, 0:1])
    rows_ref[...] = dot(wanted, mid).astype(BF16)


def base_body(mid_ref, receivers_ref, feats_ref, pr_own, pr_oth, pe_own, pe_oth, nf_own, nf_oth, base_ref, upper_ref):
    nodes, width = mid_ref.shape
    mid = mid_ref[...]
    edges = receivers_ref.shape[1]
    into = ones_where(iota((nodes, edges), 0) == receivers_ref[...])
    half = width // 2
    for k, (pr, pe, nf) in enumerate(((pr_own, pe_own, nf_own), (pr_oth, pe_oth, nf_oth))):
        at = slice(k * half, (k + 1) * half)
        recv = dot(mid, pr[...])
        high = recv.astype(BF16)
        low = (recv - high.astype(F32)).astype(BF16)
        base_ref[:, at] = (
            dot_on(into, high, 0, 0) + dot_on(into, low, 0, 0) + dot_on(feats_ref[...], pe[...], 0, 0)
        )
        upper_ref[:, at] = dot(mid, nf[0:width, :])


def node_body(rows_ref, base_ref, upper_ref, mid_ref, receivers_ref, limit_ref, gain_ref, ps_own, ps_oth, po_own, po_oth, nf_own, nf_oth, ns_own, ns_oth, out_ref):
    first = lax.axis_index("ch") == 0
    nodes, width = mid_ref.shape
    half = width // 2
    rows = rows_ref[...]
    edges = rows.shape[0]
    into = ones_where(
        (iota((nodes, edges), 0) == receivers_ref[...]) & (limit_ref[...] > 0)
    )
    agg = None
    for k, (ps, po) in enumerate(((ps_own, po_own), (ps_oth, po_oth))):
        at = slice(k * half, (k + 1) * half)
        sent = dot(rows, ps[...]).astype(BF16).astype(F32)
        act = silu(sent + base_ref[:, at]).astype(BF16)
        term = dot(dot(into, act).astype(BF16), po[...])
        agg = term if agg is None else agg + term
    agg = agg.astype(BF16)
    update = None
    for k, (nf, ns) in enumerate(((nf_own, ns_own), (nf_oth, ns_oth))):
        at = slice(k * half, (k + 1) * half)
        hidden = silu(upper_ref[:, at] + dot(agg, nf[width:, :])).astype(BF16)
        term = dot(hidden, ns[...])
        update = term if update is None else update + term
    mean = jnp.sum(update, axis=1, keepdims=True) / width
    square = jnp.sum(update * update, axis=1, keepdims=True) / width
    scale = lax.rsqrt(square - mean * mean + 1e-05)
    pick = lambda a: jnp.where(first, a[:, :half], a[:, half:])
    out_ref[...] = (
        pick(mid_ref[...]).astype(F32) + (pick(update) - mean) * scale * gain_ref[...]
    ).astype(BF16)


def per_device(
    grid_input,
    grid_senders,
    grid_lengths,
    grid_feats,
    mesh_latent,
    mesh_senders,
    mesh_receivers,
    mesh_counts,
    mesh_feats,
    embed_first,
    embed_second,
    link_sender,
    link_receiver,
    link_edge,
    link_out,
    proc_sender,
    proc_receiver,
    proc_edge,
    proc_out,
    node_first,
    node_second,
    norm_gain,
):
    bands = lax.axis_size("band")
    slab_rows = grid_input.shape[0]
    nodes, slots = grid_senders.shape
    half = link_sender.shape[1]
    width = 2 * half
    capacity = mesh_senders.shape[1]
    edges = bands * capacity
    other = lambda a: lax.ppermute(a, "ch", [(0, 1), (1, 0)])
    at = lambda b, c: 2 * b + c
    to_owner = [(at(b + 1, 0), at(b, 0)) for b in range(bands - 1)]
    to_owner += [(at(b, 1), at(b + 1, 1)) for b in range(bands - 1)]
    to_patch = [(d, s) for s, d in to_owner]
    shape = jax.ShapeDtypeStruct

    hbm = pl.BlockSpec(memory_space=pltpu.HBM)
    vmem = pl.BlockSpec(memory_space=pltpu.VMEM)
    pin = lambda a: pltpu.with_memory_space_constraint(a, pltpu.HBM)
    latent_other = other(mesh_latent)
    blocks = nodes * slots // LANES
    tail_rows = 4 * (nodes * slots // width) + blocks // 2
    tail_inputs = [pin(a) for a in (grid_senders.T, grid_lengths.reshape(1, nodes), grid_feats, mesh_senders)]
    tail, request = call(
        functools.partial(tail_body, slab_rows, width),
        (shape((tail_rows, width), BF16), shape((edges, width), BF16)),
        tail_inputs,
        in_specs=[hbm] * 4,
        out_specs=(vmem, vmem),
        scratch=[pltpu.VMEM(a.shape, a.dtype) for a in tail_inputs]
        + [pltpu.VMEM((nodes, slots), F32), pltpu.SemaphoreType.DMA((4,))],
    )
    packed = call(
        pack_body, shape((nodes + tail_rows, width), BF16), (mesh_latent, latent_other, tail)
    )
    near_packed = lax.ppermute(packed, ("band", "ch"), to_owner)
    after = lambda token, *arrays: lax.optimization_barrier((token, *arrays))[1:]
    embed_weights = after(packed, embed_first, embed_second, link_sender)
    link_receiver, link_edge, link_out, request = after(
        packed, link_receiver, link_edge, link_out, request
    )
    request = lax.all_to_all(request, "band", 0, 0, tiled=True)

    tile = slab_rows // 4
    inputs = grid_input.shape[1]
    table = call(
        functools.partial(embed_body, tile),
        shape((width, slab_rows), BF16),
        (
            *[pin(a) for a in (grid_input.T, embed_first, embed_second, link_sender)],
            *[other(w) for w in embed_weights],
        ),
        in_specs=[hbm] * 4 + [vmem] * 3,
        out_specs=vmem,
        scratch=[pltpu.VMEM((inputs, slab_rows), BF16)]
        + [pltpu.VMEM(w.shape, BF16) for w in embed_weights]
        + [pltpu.VMEM((width, n), BF16) for n in (inputs, width)]
        + [pltpu.SemaphoreType.DMA((3 + slab_rows // tile,))],
        flops=2 * slab_rows * width * (256 + width),
        moved=4 * 1024 * 1024,
    )

    link_weights = (link_receiver, other(link_receiver), link_edge, other(link_edge))
    group_slots = BLOCKS_PER_GROUP * LANES
    scratch = lambda count: [
        pltpu.VMEM((count // BLOCKS_PER_GROUP, PAYLOAD_ROWS, group_slots), BF16),
        pltpu.VMEM((count, LANES), F32),
        pltpu.VMEM((PAYLOAD_ROWS + count * LANES // slots, width), BF16),
    ]
    own = call(
        functools.partial(own_pool_body, nodes, slots),
        shape((width, nodes // 2), F32),
        (packed, table, *link_weights),
        scratch=scratch(blocks // 2),
        flops=4 * 10**9,
        moved=4 * 1024 * 1024,
    )
    own_other = other(own)
    near = call(
        functools.partial(near_pool_body, nodes, slots),
        shape((width, nodes), BF16),
        (near_packed, table, *link_weights),
        scratch=scratch(blocks) + [pltpu.VMEM((width, nodes), F32)],
        flops=4 * 10**9,
        moved=4 * 1024 * 1024,
    )
    near_back = lax.ppermute(near, ("band", "ch"), to_patch)
    near_back_other = other(near_back)

    lanes = lambda a: a.reshape(1, edges)
    mid, rows = call(
        middle_body,
        (shape((nodes, width), BF16), shape((edges, width), BF16)),
        (packed, near_back, near_back_other, own, own_other, link_out, other(link_out), request),
    )
    rows = lax.all_to_all(rows, "band", 0, 0, tiled=True)
    pairs = []
    for w in after(mid, proc_receiver, proc_edge, node_first, proc_sender, proc_out, node_second):
        pairs.append((w, other(w)))
    pr, pe, nf, ps, po, ns = pairs
    receivers = lanes(mesh_receivers)
    limit = lanes(
        mesh_counts.reshape(bands, 1) - jnp.arange(capacity, dtype=jnp.int32)[None, :]
    )
    base, upper = call(
        base_body,
        (shape((edges, width), F32), shape((nodes, width), F32)),
        (mid, receivers, mesh_feats, *pr, *pe, *nf),
    )
    return call(
        node_body,
        shape((nodes, half), BF16),
        (rows, base, upper, mid, receivers, limit, norm_gain.reshape(1, half), *ps, *po, *nf, *ns),
    )


def solution(mesh):
    rows = P(("grp", "band"), None)
    columns = P(None, ("grp", "band"))
    split = P(("grp", "band"), "ch")
    by_column = P(None, "ch")
    by_row = P("ch", None)
    in_specs = (
        rows,
        rows,
        P(("grp", "band")),
        columns,
        split,
        rows,
        rows,
        rows,
        columns,
        by_column,
        by_row,
        by_column,
        by_column,
        by_column,
        by_row,
        by_column,
        by_column,
        by_column,
        by_row,
        by_column,
        by_row,
        P("ch"),
    )
    return jax.shard_map(
        per_device, mesh=mesh, in_specs=in_specs, out_specs=split, check_vma=False
    )
```

```python
import functools

import jax
import jax.numpy as jnp
from jax import lax
from jax.experimental import pallas as pl
from jax.experimental.pallas import tpu as pltpu
from jax.sharding import PartitionSpec as P

F32 = jnp.float32
BF16 = jnp.bfloat16
LANES = 128
CHUNK = 256
SPARE = 128
PAYLOAD_ROWS = 16
BLOCKS_PER_GROUP = 8
VMEM_LIMIT = 48 * 1024 * 1024


def dot(a, b):
    return jnp.dot(a, b, preferred_element_type=F32)


def dot_on(a, b, dim_a, dim_b):
    return lax.dot_general(a, b, (((dim_a,), (dim_b,)), ((), ())), preferred_element_type=F32)


def silu(v):
    return 0.5 * v * (1.0 + jnp.tanh(0.5 * v))


def iota(shape, dim):
    return lax.broadcasted_iota(jnp.int32, shape, dim)


def ones_where(mask):
    return jnp.where(mask, 1.0, 0.0).astype(BF16)


def call(body, out_shape, args, grid_spec=None, flops=0, moved=0, scratch=(), **kw):
    whole = pl.BlockSpec(memory_space=pltpu.VMEM)
    if "in_specs" not in kw:
        kw["in_specs"] = [whole] * len(args)
        kw["out_specs"] = jax.tree.map(lambda _: whole, out_shape)
    return pl.pallas_call(
        body,
        out_shape=out_shape,
        scratch_shapes=list(scratch),
        compiler_params=pltpu.CompilerParams(vmem_limit_bytes=VMEM_LIMIT),
        cost_estimate=pl.CostEstimate(flops=flops, bytes_accessed=moved, transcendentals=0),
        **kw,
    )(*args)


def tail_body(slab_rows, width, senders_hbm, lengths_hbm, feats_hbm, mesh_hbm, le_hbm, pe_hbm, f_hbm, latent_hbm, s_hbm, l_hbm, out_ref, request_ref, edge_ref, latent_ref, early_ref, senders_ref, lengths_ref, feats_ref, mesh_ref, le_ref, pe_ref, f_ref, turned, sems):
    band = lax.axis_index("band")
    copies = fetch(
        [(senders_hbm, senders_ref), (lengths_hbm, lengths_ref), (feats_hbm, feats_ref), (mesh_hbm, mesh_ref), (le_hbm, le_ref), (pe_hbm, pe_ref), (f_hbm, f_ref), (latent_hbm, latent_ref)]
        + pack_copies((s_hbm, l_hbm), early_ref),
        sems,
    )
    for c in copies[:6]:
        c.wait()
    slots, nodes = senders_ref.shape
    turned[...] = (senders_ref[...] - (band - 1) * slab_rows).astype(F32).T
    per_row = LANES // slots
    rows = nodes // per_row
    pieces = [turned[pl.ds(j, rows, stride=per_row), :] for j in range(per_row)]
    index = jnp.concatenate(pieces, axis=1).astype(jnp.int32)
    shape = (rows, LANES)
    spread = jnp.where(
        iota((rows, nodes), 1) // per_row == iota((rows, nodes), 0),
        lengths_ref[...].astype(F32),
        0.0,
    ).astype(BF16)
    pick = ones_where(iota((nodes, LANES), 0) % per_row == iota((nodes, LANES), 1) // slots)
    used = (iota(shape, 1) % slots).astype(F32) < dot(spread, pick)
    high = jnp.where(used, index // LANES + 1, 0).astype(F32)
    low = jnp.where(used, index % LANES, 0).astype(F32)
    half = rows // 2
    feats = feats_ref[...].astype(F32)
    parts = [feats[:, k * width : (k + 1) * width] for k in range(feats.shape[1] // width)]
    places = [high[:half], low[:half], high[half:], low[half:]]
    tail = jnp.concatenate(parts + [jnp.concatenate(places, axis=1)], axis=0)
    out_ref[...] = tail.astype(BF16)
    peers, capacity = mesh_ref.shape
    edges = peers * capacity
    peer = ones_where(iota((edges, peers), 0) // capacity == iota((edges, peers), 1))
    lists = dot(peer, mesh_ref[...].astype(F32).astype(BF16))
    own_slot = iota((edges, capacity), 0) % capacity == iota((edges, capacity), 1)
    single = jnp.where(own_slot, lists, 0.0).astype(BF16)
    request_ref[:, :LANES] = dot(single, jnp.ones((capacity, LANES), BF16)).astype(BF16)
    request_ref[:, LANES:] = jnp.zeros((edges, width - LANES), BF16)
    eight = lambda ref: jnp.concatenate(
        [ref[...].astype(F32), jnp.zeros((8 - ref.shape[0], ref.shape[1]), F32)], axis=0
    )
    edge_ref[...] = jnp.concatenate([eight(le_ref), eight(pe_ref)], axis=0).astype(BF16)
    for c in copies[6:]:
        c.wait()
    rows_f, half_width = f_ref.shape
    early_ref[early_ref.shape[0] - (rows_f + 15) // 16 * 16 :, :] = jnp.concatenate(
        [f_ref[...], jnp.zeros((-rows_f % 16, half_width), BF16)], axis=0
    )


def pack_body(own_ref, other_ref, tail_ref, out_ref):
    first = lax.axis_index("ch") == 0
    nodes = own_ref.shape[0]
    own, other = own_ref[...], other_ref[...]
    out_ref[0:nodes, :] = jnp.concatenate(
        [jnp.where(first, own, other), jnp.where(first, other, own)], axis=1
    )
    out_ref[nodes:, :] = tail_ref[...]


def fetch(moves, sems):
    copies = [pltpu.make_async_copy(src, dst, sems.at[k]) for k, (src, dst) in enumerate(moves)]
    for c in copies:
        c.start()
    return copies


def embed_body(x_hbm, own_ref, oth_ref, out_ref, x_ref, first_t, joint_t, sems):
    copies = fetch([(x_hbm, x_ref)], sems)
    half = own_ref.shape[1]
    inputs = x_ref.shape[0]
    width = 2 * half
    for k, side in enumerate((own_ref, oth_ref)):
        at = slice(k * half, (k + 1) * half)
        first_t[at, :] = side[2 * width : 2 * width + inputs, :].T
        for j, l in enumerate((own_ref, oth_ref)):
            joint = dot(side[0:half, :], l[width : width + half, :])
            joint = joint + dot(side[half:width, :], l[width + half : 2 * width, :])
            joint_t[j * half : (j + 1) * half, at] = joint.astype(BF16).T
    copies[0].wait()
    hidden = silu(dot(first_t[...], x_ref[...])).astype(BF16)
    out_ref[...] = dot(joint_t[...], hidden).astype(BF16)


def running(flag16, together):
    blocks = flag16.shape[0]
    inclusive = dot(flag16, ones_where(iota((LANES, LANES), 0) <= iota((LANES, LANES), 1)))
    square = (blocks, blocks)
    earlier = iota(square, 1) < iota(square, 0)
    earlier &= iota(square, 1) // together == iota(square, 0) // together
    return inclusive + jnp.sum(dot(ones_where(earlier), flag16), axis=1, keepdims=True)


def pool_part(high, low, feats, latent, kind, slots, room, spare, step_size, table_ref, weights, payload, late, right, out_ref, midway=lambda: None):
    lr_own, lr_oth, le_own, le_oth = weights
    blocks = high.shape[0]
    nodes = latent.shape[0]
    groups = blocks // BLOCKS_PER_GROUP
    group_nodes = nodes // groups
    group_slots = BLOCKS_PER_GROUP * LANES
    width, table_rows = table_ref.shape
    per_slab = table_rows // LANES
    recv = jnp.concatenate([dot(latent, lr_own[...]), dot(latent, lr_oth[...])], axis=1)
    edge = jnp.concatenate([le_own[...], le_oth[...]], axis=1).astype(F32)[0:8]
    right[0:nodes, :] = recv.astype(BF16)
    right[nodes:, :] = jnp.concatenate(
        [edge, jnp.zeros((PAYLOAD_ROWS - 8, width), F32)], axis=0
    ).astype(BF16)
    base = (kind * per_slab + 1).astype(F32)
    local = high - base
    valid = (local >= 0.0) & (local < float(per_slab))
    flag = jnp.where(valid, 1.0, 0.0)
    rank = running(flag.astype(BF16), BLOCKS_PER_GROUP) - 1.0
    over = valid & (rank >= float(room))
    over_flag = jnp.where(over, 1.0, 0.0)
    late[...] = jnp.where(over, running(over_flag.astype(BF16), blocks) - 1.0, -1.0)
    rank = jnp.where(valid, rank, -1.0)
    spot = iota((1, group_slots), 1) // slots

    def picked(rows, start, count, columns):
        place = iota((count, LANES), 0).astype(F32) + start
        select = jnp.concatenate([ones_where(r == place) for r in rows], axis=1)
        return dot_on(columns, select, 1, 1)

    def picked_late(start, count):
        total = None
        for g in range(groups):
            at = g * BLOCKS_PER_GROUP
            rows = [late[at + k : at + k + 1, :] for k in range(BLOCKS_PER_GROUP)]
            term = picked(rows, start, count, payload[g])
            total = term if total is None else total + term
        return total

    def pooled(compact):
        count = compact.shape[1]
        own_node = ones_where(iota((nodes, count), 0).astype(F32) + 1.0 == compact[6:7, :])
        one_low = ones_where(iota((LANES, count), 0).astype(F32) == compact[5:6, :])
        row_high = compact[4:5, :]
        choose = jnp.concatenate(
            [one_low * ones_where(row_high == float(k)) for k in range(per_slab)], axis=0
        )
        terms = jnp.concatenate([own_node, compact.astype(BF16)], axis=0)
        pre = dot(table_ref[...], choose) + dot_on(right[...], terms, 0, 0)
        return dot_on(silu(pre).astype(BF16), own_node, 1, 1)

    parts = []
    for g in range(groups):
        at = g * BLOCKS_PER_GROUP
        line = lambda a: jnp.concatenate(
            [a[at + k : at + k + 1, :] for k in range(BLOCKS_PER_GROUP)], axis=1
        )
        columns = jnp.concatenate(
            [
                feats[g],
                line(local),
                line(low),
                (spot + g * group_nodes + 1).astype(F32),
                jnp.zeros((PAYLOAD_ROWS - 7, group_slots), F32),
            ],
            axis=0,
        ).astype(BF16)
        payload[g] = columns
        rows = [rank[at + k : at + k + 1, :] for k in range(BLOCKS_PER_GROUP)]
        parts.append(picked(rows, 0.0, room, columns))
    if spare:
        parts.append(picked_late(0.0, spare))
    midway()
    out_ref[...] = pooled(jnp.concatenate(parts, axis=1))
    count = jnp.sum(over_flag).astype(jnp.int32)

    @pl.loop(0, jnp.maximum(count - spare + step_size - 1, 0) // step_size)
    def _(step):
        out_ref[...] += pooled(picked_late((step * step_size + spare).astype(F32), step_size))


def unpack(packed_ref, nodes, slots):
    width = packed_ref.shape[1]
    blocks = nodes * slots // LANES
    tail = packed_ref[nodes:, :].astype(F32)
    feat_rows = tail.shape[0] - blocks // 2
    place = lambda k: tail[feat_rows:, k * LANES : (k + 1) * LANES]
    high = jnp.concatenate([place(0), place(2)], axis=0)
    low = jnp.concatenate([place(1), place(3)], axis=0)
    per_group = BLOCKS_PER_GROUP * LANES // width
    feats = []
    for g in range(blocks // BLOCKS_PER_GROUP):
        rows = [tail[4 * k : 4 * k + 4] for k in range(g * per_group, (g + 1) * per_group)]
        feats.append(jnp.concatenate(rows, axis=1))
    return high, low, feats


def own_pool_body(nodes, slots, packed_ref, table_ref, lr_own, lr_oth, le_own, le_oth, pr_hbm, nf_hbm, ps_hbm, po_hbm, ns_hbm, out_ref, pack_hbm, payload, late, right, pack_ref, sems, pack_sem):
    copies = fetch(pack_copies((pr_hbm, nf_hbm, ps_hbm, po_hbm, ns_hbm), pack_ref), sems)
    leave = pltpu.make_async_copy(pack_ref, pack_hbm, pack_sem.at[0])

    def midway():
        for c in copies:
            c.wait()
        leave.start()

    first = lax.axis_index("ch") == 0
    high, low, feats = unpack(packed_ref, nodes, slots)
    half_blocks = high.shape[0] // 2
    half_groups = len(feats) // 2
    pick = lambda a, b: jnp.where(first, a, b)
    latent = pick(packed_ref[0 : nodes // 2, :], packed_ref[nodes // 2 : nodes, :])
    pool_part(
        pick(high[:half_blocks], high[half_blocks:]),
        pick(low[:half_blocks], low[half_blocks:]),
        [pick(feats[k], feats[half_groups + k]) for k in range(half_groups)],
        latent,
        jnp.int32(1),
        slots,
        CHUNK,
        0,
        2 * CHUNK,
        table_ref,
        (lr_own, lr_oth, le_own, le_oth),
        payload,
        late,
        right,
        out_ref,
        midway,
    )
    leave.wait()


def near_pool_body(nodes, slots, packed_ref, table_ref, lr_own, lr_oth, le_own, le_oth, out_ref, payload, late, right, total):
    high, low, feats = unpack(packed_ref, nodes, slots)
    kind = 2 * lax.axis_index("ch")
    pool_part(
        high,
        low,
        feats,
        packed_ref[0:nodes, :],
        kind,
        slots,
        CHUNK,
        SPARE,
        CHUNK,
        table_ref,
        (lr_own, lr_oth, le_own, le_oth),
        payload,
        late,
        right,
        total,
    )
    out_ref[...] = total[...].astype(BF16)


def pack_copies(refs, packed_ref):
    half = packed_ref.shape[1]
    moves, top = [], 0
    for ref in refs:
        for c in range(0, ref.shape[1], half):
            target = packed_ref.at[pl.ds(top, ref.shape[0]), :]
            moves.append((ref.at[:, pl.ds(c, half)], target))
            top += ref.shape[0]
    return moves


def middle_body(packed_ref, near_ref, near_oth_ref, own_ref, own_oth_ref, lo_own, lo_oth, request_ref, mid_ref, rows_ref):
    first = lax.axis_index("ch") == 0
    half = lo_own.shape[0]
    nodes = near_ref.shape[1]
    mine, theirs = own_ref[...], own_oth_ref[...]
    flip = lambda a: jnp.concatenate([a[half:, :], a[:half, :]], axis=0)
    theirs = flip(theirs)
    total = near_ref[...].astype(F32) + flip(near_oth_ref[...]).astype(F32)
    total = total + jnp.concatenate(
        [jnp.where(first, mine, theirs), jnp.where(first, theirs, mine)], axis=1
    )
    pool = total.astype(BF16).T
    agg = dot(pool[:, :half], lo_own[...]) + dot(pool[:, half:], lo_oth[...])
    mid = (packed_ref[0:nodes, :].astype(F32) + agg).astype(BF16)
    mid_ref[...] = mid
    request = request_ref[...].astype(F32)
    wanted = ones_where(iota((request.shape[0], nodes), 1).astype(F32) == request[:, 0:1])
    rows_ref[...] = dot(wanted, mid).astype(BF16)


def base_body(mid_ref, receivers_ref, feats_ref, edge_own, edge_oth, late_own_hbm, late_oth_hbm, base_ref, upper_ref, last_own, last_oth, late_own, late_oth, sems):
    nodes, width = mid_ref.shape
    copies = []
    top = late_own.shape[0]
    for k, (source, near_by, last) in enumerate(
        ((late_own_hbm, late_own, last_own), (late_oth_hbm, late_oth, last_oth))
    ):
        copies += [
            pltpu.make_async_copy(source.at[pl.ds(0, top), :], near_by, sems.at[2 * k]),
            pltpu.make_async_copy(
                source.at[pl.ds(top, last.shape[0]), :], last, sems.at[2 * k + 1]
            ),
        ]
    for c in copies:
        c.start()
    copies[0].wait()
    copies[2].wait()
    mid = mid_ref[...]
    edges = receivers_ref.shape[1]
    into = ones_where(iota((nodes, edges), 0) == receivers_ref[...])
    half = width // 2
    for k, (edge, late) in enumerate(((edge_own, late_own), (edge_oth, late_oth))):
        at = slice(k * half, (k + 1) * half)
        recv = dot(mid, late[0:width, :])
        top = recv.astype(BF16)
        rest_of = (recv - top.astype(F32)).astype(BF16)
        pe = edge[...].astype(F32)[8 : 8 + feats_ref.shape[0]].astype(BF16)
        base_ref[:, at] = (
            dot_on(into, top, 0, 0) + dot_on(into, rest_of, 0, 0) + dot_on(feats_ref[...], pe, 0, 0)
        )
        upper_ref[:, at] = dot(mid, late[width : 2 * width, :])
    copies[1].wait()
    copies[3].wait()


def node_body(rows_ref, base_ref, upper_ref, mid_ref, receivers_ref, limit_ref, gain_ref, late_own, late_oth, out_ref):
    first = lax.axis_index("ch") == 0
    nodes, width = mid_ref.shape
    half = width // 2
    wide = lambda late, top: jnp.concatenate(
        [late[top : top + half, :], late[top + half : top + width, :]], axis=1
    )
    rows = rows_ref[...]
    edges = rows.shape[0]
    into = ones_where(
        (iota((nodes, edges), 0) == receivers_ref[...]) & (limit_ref[...] > 0)
    )
    agg = None
    for k, late in enumerate((late_own, late_oth)):
        at = slice(k * half, (k + 1) * half)
        sent = dot(rows, late[width : 2 * width, :]).astype(BF16).astype(F32)
        act = silu(sent + base_ref[:, at]).astype(BF16)
        term = dot(dot(into, act).astype(BF16), wide(late, 2 * width))
        agg = term if agg is None else agg + term
    agg = agg.astype(BF16)
    update = None
    for k, late in enumerate((late_own, late_oth)):
        at = slice(k * half, (k + 1) * half)
        hidden = silu(upper_ref[:, at] + dot(agg, late[0:width, :])).astype(BF16)
        term = dot(hidden, wide(late, 3 * width))
        update = term if update is None else update + term
    mean = jnp.sum(update, axis=1, keepdims=True) / width
    square = jnp.sum(update * update, axis=1, keepdims=True) / width
    scale = lax.rsqrt(square - mean * mean + 1e-05)
    pick = lambda a: jnp.where(first, a[:, :half], a[:, half:])
    out_ref[...] = (
        pick(mid_ref[...]).astype(F32) + (pick(update) - mean) * scale * gain_ref[...]
    ).astype(BF16)


def per_device(
    grid_input,
    grid_senders,
    grid_lengths,
    grid_feats,
    mesh_latent,
    mesh_senders,
    mesh_receivers,
    mesh_counts,
    mesh_feats,
    embed_first,
    embed_second,
    link_sender,
    link_receiver,
    link_edge,
    link_out,
    proc_sender,
    proc_receiver,
    proc_edge,
    proc_out,
    node_first,
    node_second,
    norm_gain,
):
    bands = lax.axis_size("band")
    slab_rows = grid_input.shape[0]
    nodes, slots = grid_senders.shape
    half = link_sender.shape[1]
    width = 2 * half
    capacity = mesh_senders.shape[1]
    edges = bands * capacity
    other = lambda a: lax.ppermute(a, "ch", [(0, 1), (1, 0)])
    at = lambda b, c: 2 * b + c
    to_owner = [(at(b + 1, 0), at(b, 0)) for b in range(bands - 1)]
    to_owner += [(at(b, 1), at(b + 1, 1)) for b in range(bands - 1)]
    to_patch = [(d, s) for s, d in to_owner]
    shape = jax.ShapeDtypeStruct

    hbm = pl.BlockSpec(memory_space=pltpu.HBM)
    vmem = pl.BlockSpec(memory_space=pltpu.VMEM)
    pin = lambda a: pltpu.with_memory_space_constraint(a, pltpu.HBM)
    latent_other = other(mesh_latent)
    blocks = nodes * slots // LANES
    tail_rows = 4 * (nodes * slots // width) + blocks // 2
    tail_inputs = [pin(a) for a in (grid_senders.T, grid_lengths.reshape(1, nodes), grid_feats, mesh_senders, link_edge, proc_edge, embed_first, mesh_latent, embed_second, link_sender)]
    inputs = grid_input.shape[1]
    early_rows = 2 * width + (inputs + 15) // 16 * 16
    tail, request, edge_own, latent_own, early_own = call(
        functools.partial(tail_body, slab_rows, width),
        (shape((tail_rows, width), BF16), shape((edges, width), BF16), shape((16, half), BF16), shape(mesh_latent.shape, BF16), shape((early_rows, half), BF16)),
        tail_inputs,
        in_specs=[hbm] * 10,
        out_specs=(vmem,) * 5,
        scratch=[pltpu.VMEM(a.shape, a.dtype) for a in tail_inputs[:7]]
        + [pltpu.VMEM((nodes, slots), F32), pltpu.SemaphoreType.DMA((11,))],
    )
    packed = call(
        pack_body, shape((nodes + tail_rows, width), BF16), (latent_own, latent_other, tail)
    )
    near_packed = lax.ppermute(packed, ("band", "ch"), to_owner)
    after = lambda token, *arrays: lax.optimization_barrier((token, *arrays))[1:]
    (early_out,) = after(packed, early_own)
    link_receiver, edge_own, link_out, request = after(
        packed, link_receiver, edge_own, link_out, request
    )
    request = lax.all_to_all(request, "band", 0, 0, tiled=True)

    table = call(
        embed_body,
        shape((width, slab_rows), BF16),
        (pin(grid_input.T), early_own, other(early_out)),
        in_specs=[hbm, vmem, vmem],
        out_specs=vmem,
        scratch=[pltpu.VMEM((inputs, slab_rows), BF16)]
        + [pltpu.VMEM((width, n), BF16) for n in (inputs, width)]
        + [pltpu.SemaphoreType.DMA((1,))],
        flops=2 * slab_rows * width * (256 + width),
        moved=4 * 1024 * 1024,
    )

    edge_other = other(edge_own)
    link_weights = (link_receiver, other(link_receiver), edge_own, edge_other)
    group_slots = BLOCKS_PER_GROUP * LANES
    scratch = lambda count: [
        pltpu.VMEM((count // BLOCKS_PER_GROUP, PAYLOAD_ROWS, group_slots), BF16),
        pltpu.VMEM((count, LANES), F32),
        pltpu.VMEM((PAYLOAD_ROWS + count * LANES // slots, width), BF16),
    ]
    near = call(
        functools.partial(near_pool_body, nodes, slots),
        shape((width, nodes), BF16),
        (near_packed, table, *link_weights),
        scratch=scratch(blocks) + [pltpu.VMEM((width, nodes), F32)],
        flops=4 * 10**9,
        moved=4 * 1024 * 1024,
    )
    near_back = lax.ppermute(near, ("band", "ch"), to_patch)
    weights = (proc_receiver, node_first, proc_sender, proc_out, node_second)
    own, late_own = call(
        functools.partial(own_pool_body, nodes, slots),
        (shape((width, nodes // 2), F32), pltpu.HBM((6 * width, half), BF16)),
        (*after(near, packed), table, *link_weights, *[pin(w) for w in weights]),
        in_specs=[vmem] * 6 + [hbm] * 5,
        out_specs=(vmem, hbm),
        scratch=scratch(blocks // 2)
        + [pltpu.VMEM((6 * width, half), BF16)]
        + [pltpu.SemaphoreType.DMA((7,)), pltpu.SemaphoreType.DMA((1,))],
        flops=4 * 10**9,
        moved=4 * 1024 * 1024,
    )
    own_other = other(own)
    near_back_other = other(near_back)

    lanes = lambda a: a.reshape(1, edges)
    mid, rows = call(
        middle_body,
        (
            shape((nodes, width), BF16),
            shape((edges, width), BF16),
        ),
        (
            *(packed, near_back, near_back_other, own, own_other),
            *(link_out, other(link_out), request),
        ),
    )
    late_other = pin(other(*after(mid, late_own)))
    rows = lax.all_to_all(rows, "band", 0, 0, tiled=True)
    receivers = lanes(mesh_receivers)
    limit = lanes(
        mesh_counts.reshape(bands, 1) - jnp.arange(capacity, dtype=jnp.int32)[None, :]
    )
    base, upper, last_own, last_other = call(
        base_body,
        (
            shape((edges, width), F32),
            shape((nodes, width), F32),
            *[shape((4 * width, half), BF16)] * 2,
        ),
        (mid, receivers, mesh_feats, edge_own, edge_other, pin(late_own), late_other),
        in_specs=[vmem] * 5 + [hbm] * 2,
        out_specs=(vmem,) * 4,
        scratch=[pltpu.VMEM((2 * width, half), BF16)] * 2 + [pltpu.SemaphoreType.DMA((4,))],
    )
    return call(
        node_body,
        shape((nodes, half), BF16),
        (
            *(rows, base, upper, mid, receivers, limit, norm_gain.reshape(1, half)),
            *(last_own, last_other),
        ),
    )


def solution(mesh):
    rows = P(("grp", "band"), None)
    columns = P(None, ("grp", "band"))
    split = P(("grp", "band"), "ch")
    by_column = P(None, "ch")
    by_row = P("ch", None)
    in_specs = (
        rows,
        rows,
        P(("grp", "band")),
        columns,
        split,
        rows,
        rows,
        rows,
        columns,
        by_column,
        by_row,
        by_column,
        by_column,
        by_column,
        by_row,
        by_column,
        by_column,
        by_column,
        by_row,
        by_column,
        by_row,
        P("ch"),
    )
    return jax.shard_map(
        per_device, mesh=mesh, in_specs=in_specs, out_specs=split, check_vma=False
    )
```

```python
import functools

import jax
import jax.numpy as jnp
from jax import lax
from jax.experimental import pallas as pl
from jax.experimental.pallas import tpu as pltpu
from jax.sharding import PartitionSpec as P

F32 = jnp.float32
BF16 = jnp.bfloat16
LANES = 128
CHUNK = 256
SPARE = 128
ROOM = CHUNK - SPARE // 4
PAYLOAD_ROWS = 16
BLOCKS_PER_GROUP = 8
VMEM_LIMIT = 48 * 1024 * 1024


def dot(a, b):
    return jnp.dot(a, b, preferred_element_type=F32)


def dot_on(a, b, dim_a, dim_b):
    return lax.dot_general(a, b, (((dim_a,), (dim_b,)), ((), ())), preferred_element_type=F32)


def silu(v):
    return 0.5 * v * (1.0 + jnp.tanh(0.5 * v))


def iota(shape, dim):
    return lax.broadcasted_iota(jnp.int32, shape, dim)


def ones_where(mask):
    return jnp.where(mask, 1.0, 0.0).astype(BF16)


def call(body, out_shape, args, grid_spec=None, flops=0, moved=0, scratch=(), **kw):
    whole = pl.BlockSpec(memory_space=pltpu.VMEM)
    if "in_specs" not in kw:
        kw["in_specs"] = [whole] * len(args)
        kw["out_specs"] = jax.tree.map(lambda _: whole, out_shape)
    return pl.pallas_call(
        body,
        out_shape=out_shape,
        scratch_shapes=list(scratch),
        compiler_params=pltpu.CompilerParams(vmem_limit_bytes=VMEM_LIMIT),
        cost_estimate=pl.CostEstimate(flops=flops, bytes_accessed=moved, transcendentals=0),
        **kw,
    )(*args)


def tail_body(slab_rows, width, senders_hbm, lengths_hbm, feats_hbm, mesh_hbm, le_hbm, pe_hbm, f_hbm, latent_hbm, s_hbm, l_hbm, out_ref, request_ref, edge_ref, latent_ref, early_ref, senders_ref, lengths_ref, feats_ref, mesh_ref, le_ref, pe_ref, f_ref, turned, sems):
    band = lax.axis_index("band")
    copies = fetch(
        [(senders_hbm, senders_ref), (lengths_hbm, lengths_ref), (feats_hbm, feats_ref), (mesh_hbm, mesh_ref), (le_hbm, le_ref), (pe_hbm, pe_ref), (f_hbm, f_ref), (latent_hbm, latent_ref)]
        + pack_copies((s_hbm, l_hbm), early_ref),
        sems,
    )
    for c in copies[:6]:
        c.wait()
    slots, nodes = senders_ref.shape
    turned[...] = (senders_ref[...] - (band - 1) * slab_rows).astype(F32).T
    per_row = LANES // slots
    rows = nodes // per_row
    pieces = [turned[pl.ds(j, rows, stride=per_row), :] for j in range(per_row)]
    index = jnp.concatenate(pieces, axis=1).astype(jnp.int32)
    shape = (rows, LANES)
    spread = jnp.where(
        iota((rows, nodes), 1) // per_row == iota((rows, nodes), 0),
        lengths_ref[...].astype(F32),
        0.0,
    ).astype(BF16)
    pick = ones_where(iota((nodes, LANES), 0) % per_row == iota((nodes, LANES), 1) // slots)
    used = (iota(shape, 1) % slots).astype(F32) < dot(spread, pick)
    high = jnp.where(used, index // LANES + 1, 0).astype(F32)
    low = jnp.where(used, index % LANES, 0).astype(F32)
    half = rows // 2
    feats = feats_ref[...].astype(F32)
    parts = [feats[:, k * width : (k + 1) * width] for k in range(feats.shape[1] // width)]
    places = [high[:half], low[:half], high[half:], low[half:]]
    tail = jnp.concatenate(parts + [jnp.concatenate(places, axis=1)], axis=0)
    out_ref[...] = tail.astype(BF16)
    peers, capacity = mesh_ref.shape
    edges = peers * capacity
    peer = ones_where(iota((edges, peers), 0) // capacity == iota((edges, peers), 1))
    lists = dot(peer, mesh_ref[...].astype(F32).astype(BF16))
    own_slot = iota((edges, capacity), 0) % capacity == iota((edges, capacity), 1)
    single = jnp.where(own_slot, lists, 0.0).astype(BF16)
    request_ref[:, :LANES] = dot(single, jnp.ones((capacity, LANES), BF16)).astype(BF16)
    request_ref[:, LANES:] = jnp.zeros((edges, width - LANES), BF16)
    eight = lambda ref: jnp.concatenate(
        [ref[...].astype(F32), jnp.zeros((8 - ref.shape[0], ref.shape[1]), F32)], axis=0
    )
    edge_ref[...] = jnp.concatenate([eight(le_ref), eight(pe_ref)], axis=0).astype(BF16)
    for c in copies[6:]:
        c.wait()
    rows_f, half_width = f_ref.shape
    early_ref[early_ref.shape[0] - (rows_f + 15) // 16 * 16 :, :] = jnp.concatenate(
        [f_ref[...], jnp.zeros((-rows_f % 16, half_width), BF16)], axis=0
    )


def pack_body(own_ref, other_ref, tail_ref, out_ref):
    first = lax.axis_index("ch") == 0
    nodes = own_ref.shape[0]
    own, other = own_ref[...], other_ref[...]
    out_ref[0:nodes, :] = jnp.concatenate(
        [jnp.where(first, own, other), jnp.where(first, other, own)], axis=1
    )
    out_ref[nodes:, :] = tail_ref[...]


def fetch(moves, sems):
    copies = [pltpu.make_async_copy(src, dst, sems.at[k]) for k, (src, dst) in enumerate(moves)]
    for c in copies:
        c.start()
    return copies


def embed_body(x_hbm, own_ref, oth_ref, pr_hbm, nf_hbm, ps_hbm, po_hbm, ns_hbm, out_ref, pack_hbm, x_ref, first_t, joint_t, pack_ref, sems, pack_sem):
    copies = fetch([(x_hbm, x_ref)] + pack_copies((pr_hbm, nf_hbm, ps_hbm, po_hbm, ns_hbm), pack_ref), sems)
    leave = pltpu.make_async_copy(pack_ref, pack_hbm, pack_sem.at[0])
    half = own_ref.shape[1]
    inputs = x_ref.shape[0]
    width = 2 * half
    for k, side in enumerate((own_ref, oth_ref)):
        at = slice(k * half, (k + 1) * half)
        first_t[at, :] = side[2 * width : 2 * width + inputs, :].T
        for j, l in enumerate((own_ref, oth_ref)):
            joint = dot(side[0:half, :], l[width : width + half, :])
            joint = joint + dot(side[half:width, :], l[width + half : 2 * width, :])
            joint_t[j * half : (j + 1) * half, at] = joint.astype(BF16).T
    copies[0].wait()
    hidden = silu(dot(first_t[...], x_ref[...])).astype(BF16)
    for c in copies[1:]:
        c.wait()
    leave.start()
    out_ref[...] = dot(joint_t[...], hidden).astype(BF16)
    leave.wait()


def running(flag16, together):
    blocks = flag16.shape[0]
    inclusive = dot(flag16, ones_where(iota((LANES, LANES), 0) <= iota((LANES, LANES), 1)))
    square = (blocks, blocks)
    earlier = iota(square, 1) < iota(square, 0)
    earlier &= iota(square, 1) // together == iota(square, 0) // together
    return inclusive + jnp.sum(dot(ones_where(earlier), flag16), axis=1, keepdims=True)


def pool_part(high, low, feats, latent, kind, slots, room, spare, step_size, table_ref, weights, payload, late, right, out_ref):
    lr_own, lr_oth, le_own, le_oth = weights
    blocks = high.shape[0]
    nodes = latent.shape[0]
    groups = blocks // BLOCKS_PER_GROUP
    group_nodes = nodes // groups
    group_slots = BLOCKS_PER_GROUP * LANES
    width, table_rows = table_ref.shape
    per_slab = table_rows // LANES
    recv = jnp.concatenate([dot(latent, lr_own[...]), dot(latent, lr_oth[...])], axis=1)
    edge = jnp.concatenate([le_own[...], le_oth[...]], axis=1).astype(F32)[0:8]
    right[0:nodes, :] = recv.astype(BF16)
    right[nodes:, :] = jnp.concatenate(
        [edge, jnp.zeros((PAYLOAD_ROWS - 8, width), F32)], axis=0
    ).astype(BF16)
    base = (kind * per_slab + 1).astype(F32)
    local = high - base
    valid = (local >= 0.0) & (local < float(per_slab))
    flag = jnp.where(valid, 1.0, 0.0)
    rank = running(flag.astype(BF16), BLOCKS_PER_GROUP) - 1.0
    over = valid & (rank >= float(room))
    over_flag = jnp.where(over, 1.0, 0.0)
    late[...] = jnp.where(over, running(over_flag.astype(BF16), blocks) - 1.0, -1.0)
    rank = jnp.where(valid, rank, -1.0)
    spot = iota((1, group_slots), 1) // slots

    def picked(rows, start, count, columns):
        place = iota((count, LANES), 0).astype(F32) + start
        select = jnp.concatenate([ones_where(r == place) for r in rows], axis=1)
        return dot_on(columns, select, 1, 1)

    def picked_late(start, count):
        total = None
        for g in range(groups):
            at = g * BLOCKS_PER_GROUP
            rows = [late[at + k : at + k + 1, :] for k in range(BLOCKS_PER_GROUP)]
            term = picked(rows, start, count, payload[g])
            total = term if total is None else total + term
        return total

    def pooled(compact):
        count = compact.shape[1]
        own_node = ones_where(iota((nodes, count), 0).astype(F32) + 1.0 == compact[6:7, :])
        one_low = ones_where(iota((LANES, count), 0).astype(F32) == compact[5:6, :])
        row_high = compact[4:5, :]
        choose = jnp.concatenate(
            [one_low * ones_where(row_high == float(k)) for k in range(per_slab)], axis=0
        )
        terms = jnp.concatenate([own_node, compact.astype(BF16)], axis=0)
        pre = dot(table_ref[...], choose) + dot_on(right[...], terms, 0, 0)
        return dot_on(silu(pre).astype(BF16), own_node, 1, 1)

    parts = []
    for g in range(groups):
        at = g * BLOCKS_PER_GROUP
        line = lambda a: jnp.concatenate(
            [a[at + k : at + k + 1, :] for k in range(BLOCKS_PER_GROUP)], axis=1
        )
        columns = jnp.concatenate(
            [
                feats[g],
                line(local),
                line(low),
                (spot + g * group_nodes + 1).astype(F32),
                jnp.zeros((PAYLOAD_ROWS - 7, group_slots), F32),
            ],
            axis=0,
        ).astype(BF16)
        payload[g] = columns
        rows = [rank[at + k : at + k + 1, :] for k in range(BLOCKS_PER_GROUP)]
        parts.append(picked(rows, 0.0, room, columns))
    if spare:
        parts.append(picked_late(0.0, spare))
    out_ref[...] = pooled(jnp.concatenate(parts, axis=1))
    count = jnp.sum(over_flag).astype(jnp.int32)

    @pl.loop(0, jnp.maximum(count - spare + step_size - 1, 0) // step_size)
    def _(step):
        out_ref[...] += pooled(picked_late((step * step_size + spare).astype(F32), step_size))


def unpack(packed_ref, nodes, slots):
    width = packed_ref.shape[1]
    blocks = nodes * slots // LANES
    tail = packed_ref[nodes:, :].astype(F32)
    feat_rows = tail.shape[0] - blocks // 2
    place = lambda k: tail[feat_rows:, k * LANES : (k + 1) * LANES]
    high = jnp.concatenate([place(0), place(2)], axis=0)
    low = jnp.concatenate([place(1), place(3)], axis=0)
    per_group = BLOCKS_PER_GROUP * LANES // width
    feats = []
    for g in range(blocks // BLOCKS_PER_GROUP):
        rows = [tail[4 * k : 4 * k + 4] for k in range(g * per_group, (g + 1) * per_group)]
        feats.append(jnp.concatenate(rows, axis=1))
    return high, low, feats


def place_of():
    band, core = lax.axis_index("band"), lax.axis_index("ch")
    last = lax.axis_size("band") - 1
    idle = ((core == 1) & (band == 0)) | ((core == 0) & (band == last))
    return core, idle, (band == 0) | (band == last)


def keep_nodes(high, slots, masked, parity):
    odd = iota(high.shape, 1) // slots % 2
    return jnp.where(masked & (odd != parity), 0.0, high)


def own_pool_body(nodes, slots, near_ref, packed_ref, table_ref, lr_own, lr_oth, le_own, le_oth, out_ref, payload, late, right, total):
    core, idle, edge = place_of()
    first = core == 0
    high, low, feats = unpack(packed_ref, nodes, slots)
    high = keep_nodes(high, slots, edge, 1)
    half_blocks = high.shape[0] // 2
    half_groups = len(feats) // 2
    pick = lambda a, b: jnp.where(first, a, b)
    latent = pick(packed_ref[0 : nodes // 2, :], packed_ref[nodes // 2 : nodes, :])
    pool_part(
        pick(high[:half_blocks], high[half_blocks:]),
        pick(low[:half_blocks], low[half_blocks:]),
        [pick(feats[k], feats[half_groups + k]) for k in range(half_groups)],
        latent,
        jnp.int32(1),
        slots,
        CHUNK,
        0,
        CHUNK,
        table_ref,
        (lr_own, lr_oth, le_own, le_oth),
        payload,
        late,
        right,
        total,
    )
    mine = total[...]
    none = jnp.zeros(mine.shape, F32)
    both = jnp.concatenate([pick(mine, none), pick(none, mine)], axis=1)
    out_ref[...] = (both + jnp.where(idle, near_ref[...].astype(F32), 0.0)).astype(BF16)


def near_pool_body(nodes, slots, packed_ref, own_ref, table_ref, lr_own, lr_oth, le_own, le_oth, out_ref, payload, late, right, total):
    core, idle, _ = place_of()
    own = unpack(own_ref, nodes, slots)
    near = unpack(packed_ref, nodes, slots)
    pick = lambda a, b: jnp.where(idle, a, b)
    high = pick(keep_nodes(own[0], slots, True, 0), near[0])
    low = pick(own[1], near[1])
    feats = [pick(a, b) for a, b in zip(own[2], near[2])]
    latent = pick(own_ref[0:nodes, :], packed_ref[0:nodes, :])
    kind = pick(1, 2 * core)
    pool_part(
        high,
        low,
        feats,
        latent,
        kind,
        slots,
        ROOM,
        SPARE,
        CHUNK,
        table_ref,
        (lr_own, lr_oth, le_own, le_oth),
        payload,
        late,
        right,
        total,
    )
    out_ref[...] = total[...].astype(BF16)


def pack_copies(refs, packed_ref):
    half = packed_ref.shape[1]
    moves, top = [], 0
    for ref in refs:
        for c in range(0, ref.shape[1], half):
            target = packed_ref.at[pl.ds(top, ref.shape[0]), :]
            moves.append((ref.at[:, pl.ds(c, half)], target))
            top += ref.shape[0]
    return moves


def middle_body(packed_ref, near_ref, near_oth_ref, own_ref, own_oth_ref, lo_own, lo_oth, request_ref, mid_ref, rows_ref):
    half = lo_own.shape[0]
    nodes = near_ref.shape[1]
    flip = lambda a: jnp.concatenate([a[half:, :], a[:half, :]], axis=0)
    wide = lambda a, b: a[...].astype(F32) + b[...].astype(F32)
    total = wide(near_ref, own_ref) + flip(wide(near_oth_ref, own_oth_ref))
    pool = total.astype(BF16)
    agg = dot_on(pool[:half], lo_own[...], 0, 0) + dot_on(pool[half:], lo_oth[...], 0, 0)
    mid = (packed_ref[0:nodes, :].astype(F32) + agg).astype(BF16)
    mid_ref[...] = mid
    request = request_ref[...].astype(F32)
    wanted = ones_where(iota((request.shape[0], nodes), 1).astype(F32) == request[:, 0:1])
    rows_ref[...] = dot(wanted, mid).astype(BF16)


def base_body(mid_ref, receivers_ref, feats_ref, edge_own, edge_oth, own_hbm, oth_hbm, base_ref, upper_ref, last_own, last_oth, late_own, late_oth, sems):
    nodes, width = mid_ref.shape
    top = late_own.shape[0]
    rest = last_own.shape[0]
    moves = [(own_hbm.at[pl.ds(0, top), :], late_own), (oth_hbm.at[pl.ds(0, top), :], late_oth)]
    moves += [(own_hbm.at[pl.ds(top, rest), :], last_own), (oth_hbm.at[pl.ds(top, rest), :], last_oth)]
    copies = fetch(moves, sems)
    copies[0].wait()
    copies[1].wait()
    mid = mid_ref[...]
    edges = receivers_ref.shape[1]
    into = ones_where(iota((nodes, edges), 0) == receivers_ref[...])
    half = width // 2
    for k, (edge, late) in enumerate(((edge_own, late_own), (edge_oth, late_oth))):
        at = slice(k * half, (k + 1) * half)
        recv = dot(mid, late[0:width, :])
        top = recv.astype(BF16)
        rest_of = (recv - top.astype(F32)).astype(BF16)
        pe = edge[...].astype(F32)[8 : 8 + feats_ref.shape[0]].astype(BF16)
        base_ref[:, at] = (
            dot_on(into, top, 0, 0) + dot_on(into, rest_of, 0, 0) + dot_on(feats_ref[...], pe, 0, 0)
        )
        upper_ref[:, at] = dot(mid, late[width : 2 * width, :])
    for c in copies[2:]:
        c.wait()


def node_body(rows_ref, base_ref, upper_ref, mid_ref, receivers_ref, limit_ref, gain_ref, late_own, late_oth, out_ref):
    first = lax.axis_index("ch") == 0
    nodes, width = mid_ref.shape
    half = width // 2
    wide = lambda late, top: jnp.concatenate(
        [late[top : top + half, :], late[top + half : top + width, :]], axis=1
    )
    rows = rows_ref[...]
    edges = rows.shape[0]
    into = ones_where(
        (iota((nodes, edges), 0) == receivers_ref[...]) & (limit_ref[...] > 0)
    )
    agg = None
    for k, late in enumerate((late_own, late_oth)):
        at = slice(k * half, (k + 1) * half)
        sent = dot(rows, late[width : 2 * width, :]).astype(BF16).astype(F32)
        act = silu(sent + base_ref[:, at]).astype(BF16)
        term = dot(dot(into, act).astype(BF16), wide(late, 2 * width))
        agg = term if agg is None else agg + term
    agg = agg.astype(BF16)
    update = None
    for k, late in enumerate((late_own, late_oth)):
        at = slice(k * half, (k + 1) * half)
        hidden = silu(upper_ref[:, at] + dot(agg, late[0:width, :])).astype(BF16)
        term = dot(hidden, wide(late, 3 * width))
        update = term if update is None else update + term
    mean = jnp.sum(update, axis=1, keepdims=True) / width
    square = jnp.sum(update * update, axis=1, keepdims=True) / width
    scale = lax.rsqrt(square - mean * mean + 1e-05)
    pick = lambda a: jnp.where(first, a[:, :half], a[:, half:])
    out_ref[...] = (
        pick(mid_ref[...]).astype(F32) + (pick(update) - mean) * scale * gain_ref[...]
    ).astype(BF16)


def per_device(
    grid_input,
    grid_senders,
    grid_lengths,
    grid_feats,
    mesh_latent,
    mesh_senders,
    mesh_receivers,
    mesh_counts,
    mesh_feats,
    embed_first,
    embed_second,
    link_sender,
    link_receiver,
    link_edge,
    link_out,
    proc_sender,
    proc_receiver,
    proc_edge,
    proc_out,
    node_first,
    node_second,
    norm_gain,
):
    bands = lax.axis_size("band")
    slab_rows = grid_input.shape[0]
    nodes, slots = grid_senders.shape
    half = link_sender.shape[1]
    width = 2 * half
    capacity = mesh_senders.shape[1]
    edges = bands * capacity
    other = lambda a: lax.ppermute(a, "ch", [(0, 1), (1, 0)])
    at = lambda b, c: 2 * b + c
    to_owner = [(at(b + 1, 0), at(b, 0)) for b in range(bands - 1)]
    to_owner += [(at(b, 1), at(b + 1, 1)) for b in range(bands - 1)]
    to_patch = [(d, s) for s, d in to_owner]
    shape = jax.ShapeDtypeStruct

    hbm = pl.BlockSpec(memory_space=pltpu.HBM)
    vmem = pl.BlockSpec(memory_space=pltpu.VMEM)
    pin = lambda a: pltpu.with_memory_space_constraint(a, pltpu.HBM)
    latent_other = other(mesh_latent)
    blocks = nodes * slots // LANES
    tail_rows = 4 * (nodes * slots // width) + blocks // 2
    tail_inputs = [pin(a) for a in (grid_senders.T, grid_lengths.reshape(1, nodes), grid_feats, mesh_senders, link_edge, proc_edge, embed_first, mesh_latent, embed_second, link_sender)]
    inputs = grid_input.shape[1]
    early_rows = 2 * width + (inputs + 15) // 16 * 16
    tail, request, edge_own, latent_own, early_own = call(
        functools.partial(tail_body, slab_rows, width),
        (shape((tail_rows, width), BF16), shape((edges, width), BF16), shape((16, half), BF16), shape(mesh_latent.shape, BF16), shape((early_rows, half), BF16)),
        tail_inputs,
        in_specs=[hbm] * 10,
        out_specs=(vmem,) * 5,
        scratch=[pltpu.VMEM(a.shape, a.dtype) for a in tail_inputs[:7]]
        + [pltpu.VMEM((nodes, slots), F32), pltpu.SemaphoreType.DMA((11,))],
    )
    packed = call(
        pack_body, shape((nodes + tail_rows, width), BF16), (latent_own, latent_other, tail)
    )
    near_packed = lax.ppermute(packed, ("band", "ch"), to_owner)
    after = lambda token, *arrays: lax.optimization_barrier((token, *arrays))[1:]
    (early_out,) = after(packed, early_own)
    link_receiver, edge_own, link_out, request = after(
        packed, link_receiver, edge_own, link_out, request
    )
    request = lax.all_to_all(request, "band", 0, 0, tiled=True)

    table, late = call(
        embed_body,
        (shape((width, slab_rows), BF16), pltpu.HBM((6 * width, half), BF16)),
        (
            *(pin(grid_input.T), early_own, other(early_out)),
            *[pin(w) for w in (proc_receiver, node_first, proc_sender, proc_out, node_second)],
        ),
        in_specs=[hbm, vmem, vmem] + [hbm] * 5,
        out_specs=(vmem, hbm),
        scratch=[pltpu.VMEM((inputs, slab_rows), BF16)]
        + [pltpu.VMEM((width, n), BF16) for n in (inputs, width)]
        + [pltpu.VMEM((6 * width, half), BF16)]
        + [pltpu.SemaphoreType.DMA((8,)), pltpu.SemaphoreType.DMA((1,))],
        flops=2 * slab_rows * width * (256 + width),
        moved=4 * 1024 * 1024,
    )

    edge_other = other(edge_own)
    link_weights = (link_receiver, other(link_receiver), edge_own, edge_other)
    group_slots = BLOCKS_PER_GROUP * LANES
    scratch = lambda count: [
        pltpu.VMEM((count // BLOCKS_PER_GROUP, PAYLOAD_ROWS, group_slots), BF16),
        pltpu.VMEM((count, LANES), F32),
        pltpu.VMEM((PAYLOAD_ROWS + count * LANES // slots, width), BF16),
    ]
    near = call(
        functools.partial(near_pool_body, nodes, slots),
        shape((width, nodes), BF16),
        (near_packed, packed, table, *link_weights),
        scratch=scratch(blocks) + [pltpu.VMEM((width, nodes), F32)],
        flops=4 * 10**9,
        moved=4 * 1024 * 1024,
    )
    near_back = lax.ppermute(near, ("band", "ch"), to_patch)
    own = call(
        functools.partial(own_pool_body, nodes, slots),
        shape((width, nodes), BF16),
        (near, packed, table, *link_weights),
        scratch=scratch(blocks // 2) + [pltpu.VMEM((width, nodes // 2), F32)],
        flops=4 * 10**9,
        moved=4 * 1024 * 1024,
    )
    own_other = other(own)
    near_back_other = other(near_back)

    lanes = lambda a: a.reshape(1, edges)
    mid, rows = call(
        middle_body,
        (
            shape((nodes, width), BF16),
            shape((edges, width), BF16),
        ),
        (
            *(packed, near_back, near_back_other, own, own_other),
            *(link_out, other(link_out), request),
        ),
    )
    late_other = pin(other(*after(mid, late)))
    rows = lax.all_to_all(rows, "band", 0, 0, tiled=True)
    receivers = lanes(mesh_receivers)
    limit = lanes(
        mesh_counts.reshape(bands, 1) - jnp.arange(capacity, dtype=jnp.int32)[None, :]
    )
    base, upper, last_own, last_other = call(
        base_body,
        (
            shape((edges, width), F32),
            shape((nodes, width), F32),
            *[shape((4 * width, half), BF16)] * 2,
        ),
        (mid, receivers, mesh_feats, edge_own, edge_other, pin(late), late_other),
        in_specs=[vmem] * 5 + [hbm] * 2,
        out_specs=(vmem,) * 4,
        scratch=[pltpu.VMEM((2 * width, half), BF16)] * 2 + [pltpu.SemaphoreType.DMA((4,))],
    )
    return call(
        node_body,
        shape((nodes, half), BF16),
        (
            *(rows, base, upper, mid, receivers, limit, norm_gain.reshape(1, half)),
            *(last_own, last_other),
        ),
    )


def solution(mesh):
    rows = P(("grp", "band"), None)
    columns = P(None, ("grp", "band"))
    split = P(("grp", "band"), "ch")
    by_column = P(None, "ch")
    by_row = P("ch", None)
    in_specs = (
        rows,
        rows,
        P(("grp", "band")),
        columns,
        split,
        rows,
        rows,
        rows,
        columns,
        by_column,
        by_row,
        by_column,
        by_column,
        by_column,
        by_row,
        by_column,
        by_column,
        by_column,
        by_row,
        by_column,
        by_row,
        P("ch"),
    )
    return jax.shard_map(
        per_device, mesh=mesh, in_specs=in_specs, out_specs=split, check_vma=False
    )
```

```python
import functools

import jax
import jax.numpy as jnp
from jax import lax
from jax.experimental import pallas as pl
from jax.experimental.pallas import tpu as pltpu
from jax.sharding import PartitionSpec as P

F32 = jnp.float32
BF16 = jnp.bfloat16
LANES = 128
CHUNK = 256
SPARE = 128
ROOM = CHUNK - SPARE // 4
PAYLOAD_ROWS = 16
BLOCKS_PER_GROUP = 8
VMEM_LIMIT = 48 * 1024 * 1024


def dot(a, b):
    return jnp.dot(a, b, preferred_element_type=F32)


def dot_on(a, b, dim_a, dim_b):
    return lax.dot_general(a, b, (((dim_a,), (dim_b,)), ((), ())), preferred_element_type=F32)


def silu(v):
    return 0.5 * v * (1.0 + jnp.tanh(0.5 * v))


def iota(shape, dim):
    return lax.broadcasted_iota(jnp.int32, shape, dim)


def ones_where(mask):
    return jnp.where(mask, 1.0, 0.0).astype(BF16)


def call(body, out_shape, args, grid_spec=None, flops=0, moved=0, scratch=(), **kw):
    whole = pl.BlockSpec(memory_space=pltpu.VMEM)
    if "in_specs" not in kw:
        kw["in_specs"] = [whole] * len(args)
        kw["out_specs"] = jax.tree.map(lambda _: whole, out_shape)
    return pl.pallas_call(
        body,
        out_shape=out_shape,
        scratch_shapes=list(scratch),
        compiler_params=pltpu.CompilerParams(vmem_limit_bytes=VMEM_LIMIT),
        cost_estimate=pl.CostEstimate(flops=flops, bytes_accessed=moved, transcendentals=0),
        **kw,
    )(*args)


def tail_body(slab_rows, width, senders_hbm, lengths_hbm, feats_hbm, mesh_hbm, le_hbm, pe_hbm, f_hbm, latent_hbm, s_hbm, l_hbm, out_ref, request_hbm, edge_ref, latent_ref, early_ref, senders_ref, lengths_ref, feats_ref, mesh_ref, le_ref, pe_ref, f_ref, turned, request_ref, sems, request_sem):
    band = lax.axis_index("band")
    copies = fetch(
        [(senders_hbm, senders_ref), (lengths_hbm, lengths_ref), (feats_hbm, feats_ref), (mesh_hbm, mesh_ref), (le_hbm, le_ref), (pe_hbm, pe_ref), (f_hbm, f_ref), (latent_hbm, latent_ref)]
        + pack_copies((s_hbm, l_hbm), early_ref),
        sems,
    )
    for c in copies[:6]:
        c.wait()
    peers, capacity = mesh_ref.shape
    edges = peers * capacity
    peer = ones_where(iota((edges, peers), 0) // capacity == iota((edges, peers), 1))
    lists = dot(peer, mesh_ref[...].astype(F32).astype(BF16))
    own_slot = iota((edges, capacity), 0) % capacity == iota((edges, capacity), 1)
    single = jnp.where(own_slot, lists, 0.0).astype(BF16)
    request_ref[:, :LANES] = dot(single, jnp.ones((capacity, LANES), BF16)).astype(BF16)
    request_ref[:, LANES:] = jnp.zeros((edges, width - LANES), BF16)
    leave = pltpu.make_async_copy(request_ref, request_hbm, request_sem.at[0])
    leave.start()
    slots, nodes = senders_ref.shape
    turned[...] = (senders_ref[...] - (band - 1) * slab_rows).astype(F32).T
    per_row = LANES // slots
    rows = nodes // per_row
    pieces = [turned[pl.ds(j, rows, stride=per_row), :] for j in range(per_row)]
    index = jnp.concatenate(pieces, axis=1).astype(jnp.int32)
    shape = (rows, LANES)
    spread = jnp.where(
        iota((rows, nodes), 1) // per_row == iota((rows, nodes), 0),
        lengths_ref[...].astype(F32),
        0.0,
    ).astype(BF16)
    pick = ones_where(iota((nodes, LANES), 0) % per_row == iota((nodes, LANES), 1) // slots)
    used = (iota(shape, 1) % slots).astype(F32) < dot(spread, pick)
    high = jnp.where(used, index // LANES + 1, 0).astype(F32)
    low = jnp.where(used, index % LANES, 0).astype(F32)
    half = rows // 2
    feats = feats_ref[...].astype(F32)
    parts = [feats[:, k * width : (k + 1) * width] for k in range(feats.shape[1] // width)]
    places = [high[:half], low[:half], high[half:], low[half:]]
    tail = jnp.concatenate(parts + [jnp.concatenate(places, axis=1)], axis=0)
    out_ref[...] = tail.astype(BF16)
    eight = lambda ref: jnp.concatenate(
        [ref[...].astype(F32), jnp.zeros((8 - ref.shape[0], ref.shape[1]), F32)], axis=0
    )
    edge_ref[...] = jnp.concatenate([eight(le_ref), eight(pe_ref)], axis=0).astype(BF16)
    for c in copies[6:]:
        c.wait()
    rows_f, half_width = f_ref.shape
    early_ref[early_ref.shape[0] - (rows_f + 15) // 16 * 16 :, :] = jnp.concatenate(
        [f_ref[...], jnp.zeros((-rows_f % 16, half_width), BF16)], axis=0
    )
    leave.wait()


def pack_body(own_ref, other_ref, tail_ref, out_ref):
    first = lax.axis_index("ch") == 0
    nodes = own_ref.shape[0]
    own, other = own_ref[...], other_ref[...]
    out_ref[0:nodes, :] = jnp.concatenate(
        [jnp.where(first, own, other), jnp.where(first, other, own)], axis=1
    )
    out_ref[nodes:, :] = tail_ref[...]


def fetch(moves, sems):
    copies = [pltpu.make_async_copy(src, dst, sems.at[k]) for k, (src, dst) in enumerate(moves)]
    for c in copies:
        c.start()
    return copies


def embed_body(x_hbm, own_ref, oth_ref, pr_hbm, nf_hbm, ps_hbm, po_hbm, ns_hbm, out_ref, pack_hbm, x_ref, first_t, joint_t, pack_ref, sems, pack_sem):
    copies = fetch([(x_hbm, x_ref)] + pack_copies((pr_hbm, nf_hbm, ps_hbm, po_hbm, ns_hbm), pack_ref), sems)
    leave = pltpu.make_async_copy(pack_ref, pack_hbm, pack_sem.at[0])
    half = own_ref.shape[1]
    inputs = x_ref.shape[0]
    width = 2 * half
    for k, side in enumerate((own_ref, oth_ref)):
        at = slice(k * half, (k + 1) * half)
        first_t[at, :] = side[2 * width : 2 * width + inputs, :].T
        for j, l in enumerate((own_ref, oth_ref)):
            joint = dot(side[0:half, :], l[width : width + half, :])
            joint = joint + dot(side[half:width, :], l[width + half : 2 * width, :])
            joint_t[j * half : (j + 1) * half, at] = joint.astype(BF16).T
    copies[0].wait()
    hidden = silu(dot(first_t[...], x_ref[...])).astype(BF16)
    for c in copies[1:]:
        c.wait()
    leave.start()
    out_ref[...] = dot(joint_t[...], hidden).astype(BF16)
    leave.wait()


def running(flag16, together):
    blocks = flag16.shape[0]
    inclusive = dot(flag16, ones_where(iota((LANES, LANES), 0) <= iota((LANES, LANES), 1)))
    square = (blocks, blocks)
    earlier = iota(square, 1) < iota(square, 0)
    earlier &= iota(square, 1) // together == iota(square, 0) // together
    return inclusive + jnp.sum(dot(ones_where(earlier), flag16), axis=1, keepdims=True)


def pool_part(high, low, feats, latent, kind, slots, room, spare, step_size, table_ref, weights, payload, late, right, out_ref):
    lr_own, lr_oth, le_own, le_oth = weights
    blocks = high.shape[0]
    nodes = latent.shape[0]
    groups = blocks // BLOCKS_PER_GROUP
    group_nodes = nodes // groups
    group_slots = BLOCKS_PER_GROUP * LANES
    width, table_rows = table_ref.shape
    per_slab = table_rows // LANES
    recv = jnp.concatenate([dot(latent, lr_own[...]), dot(latent, lr_oth[...])], axis=1)
    edge = jnp.concatenate([le_own[...], le_oth[...]], axis=1).astype(F32)[0:8]
    right[0:nodes, :] = recv.astype(BF16)
    right[nodes:, :] = jnp.concatenate(
        [edge, jnp.zeros((PAYLOAD_ROWS - 8, width), F32)], axis=0
    ).astype(BF16)
    base = (kind * per_slab + 1).astype(F32)
    local = high - base
    valid = (local >= 0.0) & (local < float(per_slab))
    flag = jnp.where(valid, 1.0, 0.0)
    rank = running(flag.astype(BF16), BLOCKS_PER_GROUP) - 1.0
    over = valid & (rank >= float(room))
    over_flag = jnp.where(over, 1.0, 0.0)
    late[...] = jnp.where(over, running(over_flag.astype(BF16), blocks) - 1.0, -1.0)
    rank = jnp.where(valid, rank, -1.0)
    spot = iota((1, group_slots), 1) // slots

    def picked(rows, start, count, columns):
        place = iota((count, LANES), 0).astype(F32) + start
        select = jnp.concatenate([ones_where(r == place) for r in rows], axis=1)
        return dot_on(columns, select, 1, 1)

    def picked_late(start, count):
        total = None
        for g in range(groups):
            at = g * BLOCKS_PER_GROUP
            rows = [late[at + k : at + k + 1, :] for k in range(BLOCKS_PER_GROUP)]
            term = picked(rows, start, count, payload[g])
            total = term if total is None else total + term
        return total

    def pooled(compact):
        count = compact.shape[1]
        own_node = ones_where(iota((nodes, count), 0).astype(F32) + 1.0 == compact[6:7, :])
        one_low = ones_where(iota((LANES, count), 0).astype(F32) == compact[5:6, :])
        row_high = compact[4:5, :]
        choose = jnp.concatenate(
            [one_low * ones_where(row_high == float(k)) for k in range(per_slab)], axis=0
        )
        terms = jnp.concatenate([own_node, compact.astype(BF16)], axis=0)
        pre = dot(table_ref[...], choose) + dot_on(right[...], terms, 0, 0)
        return dot_on(silu(pre).astype(BF16), own_node, 1, 1)

    parts = []
    for g in range(groups):
        at = g * BLOCKS_PER_GROUP
        line = lambda a: jnp.concatenate(
            [a[at + k : at + k + 1, :] for k in range(BLOCKS_PER_GROUP)], axis=1
        )
        columns = jnp.concatenate(
            [
                feats[g],
                line(local),
                line(low),
                (spot + g * group_nodes + 1).astype(F32),
                jnp.zeros((PAYLOAD_ROWS - 7, group_slots), F32),
            ],
            axis=0,
        ).astype(BF16)
        payload[g] = columns
        rows = [rank[at + k : at + k + 1, :] for k in range(BLOCKS_PER_GROUP)]
        parts.append(picked(rows, 0.0, room, columns))
    if spare:
        parts.append(picked_late(0.0, spare))
    out_ref[...] = pooled(jnp.concatenate(parts, axis=1))
    count = jnp.sum(over_flag).astype(jnp.int32)

    @pl.loop(0, jnp.maximum(count - spare + step_size - 1, 0) // step_size)
    def _(step):
        out_ref[...] += pooled(picked_late((step * step_size + spare).astype(F32), step_size))


def unpack(packed_ref, nodes, slots):
    width = packed_ref.shape[1]
    blocks = nodes * slots // LANES
    tail = packed_ref[nodes:, :].astype(F32)
    feat_rows = tail.shape[0] - blocks // 2
    place = lambda k: tail[feat_rows:, k * LANES : (k + 1) * LANES]
    high = jnp.concatenate([place(0), place(2)], axis=0)
    low = jnp.concatenate([place(1), place(3)], axis=0)
    per_group = BLOCKS_PER_GROUP * LANES // width
    feats = []
    for g in range(blocks // BLOCKS_PER_GROUP):
        rows = [tail[4 * k : 4 * k + 4] for k in range(g * per_group, (g + 1) * per_group)]
        feats.append(jnp.concatenate(rows, axis=1))
    return high, low, feats


def place_of():
    band, core = lax.axis_index("band"), lax.axis_index("ch")
    last = lax.axis_size("band") - 1
    idle = ((core == 1) & (band == 0)) | ((core == 0) & (band == last))
    return core, idle, (band == 0) | (band == last)


def keep_nodes(high, slots, masked, parity):
    odd = iota(high.shape, 1) // slots % 2
    return jnp.where(masked & (odd != parity), 0.0, high)


def own_pool_body(nodes, slots, near_ref, packed_ref, table_ref, lr_own, lr_oth, le_own, le_oth, out_ref, payload, late, right, total):
    core, idle, edge = place_of()
    first = core == 0
    high, low, feats = unpack(packed_ref, nodes, slots)
    high = keep_nodes(high, slots, edge, 1)
    half_blocks = high.shape[0] // 2
    half_groups = len(feats) // 2
    pick = lambda a, b: jnp.where(first, a, b)
    latent = pick(packed_ref[0 : nodes // 2, :], packed_ref[nodes // 2 : nodes, :])
    pool_part(
        pick(high[:half_blocks], high[half_blocks:]),
        pick(low[:half_blocks], low[half_blocks:]),
        [pick(feats[k], feats[half_groups + k]) for k in range(half_groups)],
        latent,
        jnp.int32(1),
        slots,
        CHUNK,
        0,
        CHUNK,
        table_ref,
        (lr_own, lr_oth, le_own, le_oth),
        payload,
        late,
        right,
        total,
    )
    mine = total[...]
    none = jnp.zeros(mine.shape, F32)
    both = jnp.concatenate([pick(mine, none), pick(none, mine)], axis=1)
    out_ref[...] = (both + jnp.where(idle, near_ref[...].astype(F32), 0.0)).astype(BF16)


def near_pool_body(nodes, slots, packed_ref, own_ref, table_ref, lr_own, lr_oth, le_own, le_oth, out_ref, payload, late, right, total):
    core, idle, _ = place_of()
    own = unpack(own_ref, nodes, slots)
    near = unpack(packed_ref, nodes, slots)
    pick = lambda a, b: jnp.where(idle, a, b)
    high = pick(keep_nodes(own[0], slots, True, 0), near[0])
    low = pick(own[1], near[1])
    feats = [pick(a, b) for a, b in zip(own[2], near[2])]
    latent = pick(own_ref[0:nodes, :], packed_ref[0:nodes, :])
    kind = pick(1, 2 * core)
    pool_part(
        high,
        low,
        feats,
        latent,
        kind,
        slots,
        ROOM,
        SPARE,
        CHUNK,
        table_ref,
        (lr_own, lr_oth, le_own, le_oth),
        payload,
        late,
        right,
        total,
    )
    out_ref[...] = total[...].astype(BF16)


def pack_copies(refs, packed_ref):
    half = packed_ref.shape[1]
    moves, top = [], 0
    for ref in refs:
        for c in range(0, ref.shape[1], half):
            target = packed_ref.at[pl.ds(top, ref.shape[0]), :]
            moves.append((ref.at[:, pl.ds(c, half)], target))
            top += ref.shape[0]
    return moves


def middle_body(packed_ref, near_ref, near_oth_ref, own_ref, own_oth_ref, lo_own, lo_oth, request_ref, mid_ref, rows_ref):
    half = lo_own.shape[0]
    nodes = near_ref.shape[1]
    flip = lambda a: jnp.concatenate([a[half:, :], a[:half, :]], axis=0)
    wide = lambda a, b: a[...].astype(F32) + b[...].astype(F32)
    total = wide(near_ref, own_ref) + flip(wide(near_oth_ref, own_oth_ref))
    pool = total.astype(BF16)
    agg = dot_on(pool[:half], lo_own[...], 0, 0) + dot_on(pool[half:], lo_oth[...], 0, 0)
    mid = (packed_ref[0:nodes, :].astype(F32) + agg).astype(BF16)
    mid_ref[...] = mid
    request = request_ref[...].astype(F32)
    wanted = ones_where(iota((request.shape[0], nodes), 1).astype(F32) == request[:, 0:1])
    rows_ref[...] = dot(wanted, mid).astype(BF16)


def base_body(mid_ref, receivers_ref, feats_ref, edge_own, edge_oth, own_hbm, oth_hbm, base_ref, upper_ref, last_own, last_oth, late_own, late_oth, sems):
    nodes, width = mid_ref.shape
    top = late_own.shape[0]
    rest = last_own.shape[0]
    moves = [(own_hbm.at[pl.ds(0, top), :], late_own), (oth_hbm.at[pl.ds(0, top), :], late_oth)]
    moves += [(own_hbm.at[pl.ds(top, rest), :], last_own), (oth_hbm.at[pl.ds(top, rest), :], last_oth)]
    copies = fetch(moves, sems)
    copies[0].wait()
    copies[1].wait()
    mid = mid_ref[...]
    edges = receivers_ref.shape[1]
    into = ones_where(iota((nodes, edges), 0) == receivers_ref[...])
    half = width // 2
    for k, (edge, late) in enumerate(((edge_own, late_own), (edge_oth, late_oth))):
        at = slice(k * half, (k + 1) * half)
        recv = dot(mid, late[0:width, :])
        top = recv.astype(BF16)
        rest_of = (recv - top.astype(F32)).astype(BF16)
        pe = edge[...].astype(F32)[8 : 8 + feats_ref.shape[0]].astype(BF16)
        base_ref[:, at] = (
            dot_on(into, top, 0, 0) + dot_on(into, rest_of, 0, 0) + dot_on(feats_ref[...], pe, 0, 0)
        )
        upper_ref[:, at] = dot(mid, late[width : 2 * width, :])
    for c in copies[2:]:
        c.wait()


def node_body(rows_ref, base_ref, upper_ref, mid_ref, receivers_ref, limit_ref, gain_ref, late_own, late_oth, out_ref):
    first = lax.axis_index("ch") == 0
    nodes, width = mid_ref.shape
    half = width // 2
    wide = lambda late, top: jnp.concatenate(
        [late[top : top + half, :], late[top + half : top + width, :]], axis=1
    )
    rows = rows_ref[...]
    edges = rows.shape[0]
    into = ones_where(
        (iota((nodes, edges), 0) == receivers_ref[...]) & (limit_ref[...] > 0)
    )
    agg = None
    for k, late in enumerate((late_own, late_oth)):
        at = slice(k * half, (k + 1) * half)
        sent = dot(rows, late[width : 2 * width, :]).astype(BF16).astype(F32)
        act = silu(sent + base_ref[:, at]).astype(BF16)
        term = dot(dot(into, act).astype(BF16), wide(late, 2 * width))
        agg = term if agg is None else agg + term
    agg = agg.astype(BF16)
    update = None
    for k, late in enumerate((late_own, late_oth)):
        at = slice(k * half, (k + 1) * half)
        hidden = silu(upper_ref[:, at] + dot(agg, late[0:width, :])).astype(BF16)
        term = dot(hidden, wide(late, 3 * width))
        update = term if update is None else update + term
    mean = jnp.sum(update, axis=1, keepdims=True) / width
    square = jnp.sum(update * update, axis=1, keepdims=True) / width
    scale = lax.rsqrt(square - mean * mean + 1e-05)
    pick = lambda a: jnp.where(first, a[:, :half], a[:, half:])
    out_ref[...] = (
        pick(mid_ref[...]).astype(F32) + (pick(update) - mean) * scale * gain_ref[...]
    ).astype(BF16)


def per_device(
    grid_input,
    grid_senders,
    grid_lengths,
    grid_feats,
    mesh_latent,
    mesh_senders,
    mesh_receivers,
    mesh_counts,
    mesh_feats,
    embed_first,
    embed_second,
    link_sender,
    link_receiver,
    link_edge,
    link_out,
    proc_sender,
    proc_receiver,
    proc_edge,
    proc_out,
    node_first,
    node_second,
    norm_gain,
):
    bands = lax.axis_size("band")
    slab_rows = grid_input.shape[0]
    nodes, slots = grid_senders.shape
    half = link_sender.shape[1]
    width = 2 * half
    capacity = mesh_senders.shape[1]
    edges = bands * capacity
    other = lambda a: lax.ppermute(a, "ch", [(0, 1), (1, 0)])
    at = lambda b, c: 2 * b + c
    to_owner = [(at(b + 1, 0), at(b, 0)) for b in range(bands - 1)]
    to_owner += [(at(b, 1), at(b + 1, 1)) for b in range(bands - 1)]
    to_patch = [(d, s) for s, d in to_owner]
    shape = jax.ShapeDtypeStruct

    hbm = pl.BlockSpec(memory_space=pltpu.HBM)
    vmem = pl.BlockSpec(memory_space=pltpu.VMEM)
    pin = lambda a: pltpu.with_memory_space_constraint(a, pltpu.HBM)
    latent_other = other(mesh_latent)
    blocks = nodes * slots // LANES
    tail_rows = 4 * (nodes * slots // width) + blocks // 2
    tail_inputs = [pin(a) for a in (grid_senders.T, grid_lengths.reshape(1, nodes), grid_feats, mesh_senders, link_edge, proc_edge, embed_first, mesh_latent, embed_second, link_sender)]
    inputs = grid_input.shape[1]
    early_rows = 2 * width + (inputs + 15) // 16 * 16
    tail, request, edge_own, latent_own, early_own = call(
        functools.partial(tail_body, slab_rows, width),
        (shape((tail_rows, width), BF16), pltpu.HBM((edges, width), BF16), shape((16, half), BF16), shape(mesh_latent.shape, BF16), shape((early_rows, half), BF16)),
        tail_inputs,
        in_specs=[hbm] * 10,
        out_specs=(vmem, hbm, vmem, vmem, vmem),
        scratch=[pltpu.VMEM(a.shape, a.dtype) for a in tail_inputs[:7]]
        + [pltpu.VMEM((nodes, slots), F32), pltpu.VMEM((edges, width), BF16)]
        + [pltpu.SemaphoreType.DMA((11,)), pltpu.SemaphoreType.DMA((1,))],
    )
    packed = call(
        pack_body, shape((nodes + tail_rows, width), BF16), (latent_own, latent_other, tail)
    )
    near_packed = lax.ppermute(packed, ("band", "ch"), to_owner)
    after = lambda token, *arrays: lax.optimization_barrier((token, *arrays))[1:]
    (early_out,) = after(packed, early_own)
    link_receiver, edge_own, request = after(packed, link_receiver, edge_own, request)
    request = lax.all_to_all(request, "band", 0, 0, tiled=True)

    table, late = call(
        embed_body,
        (shape((width, slab_rows), BF16), pltpu.HBM((6 * width, half), BF16)),
        (
            *(pin(grid_input.T), early_own, other(early_out)),
            *[pin(w) for w in (proc_receiver, node_first, proc_sender, proc_out, node_second)],
        ),
        in_specs=[hbm, vmem, vmem] + [hbm] * 5,
        out_specs=(vmem, hbm),
        scratch=[pltpu.VMEM((inputs, slab_rows), BF16)]
        + [pltpu.VMEM((width, n), BF16) for n in (inputs, width)]
        + [pltpu.VMEM((6 * width, half), BF16)]
        + [pltpu.SemaphoreType.DMA((8,)), pltpu.SemaphoreType.DMA((1,))],
        flops=2 * slab_rows * width * (256 + width),
        moved=4 * 1024 * 1024,
    )

    edge_other = other(edge_own)
    link_weights = (link_receiver, other(link_receiver), edge_own, edge_other)
    group_slots = BLOCKS_PER_GROUP * LANES
    scratch = lambda count: [
        pltpu.VMEM((count // BLOCKS_PER_GROUP, PAYLOAD_ROWS, group_slots), BF16),
        pltpu.VMEM((count, LANES), F32),
        pltpu.VMEM((PAYLOAD_ROWS + count * LANES // slots, width), BF16),
    ]
    near = call(
        functools.partial(near_pool_body, nodes, slots),
        shape((width, nodes), BF16),
        (near_packed, packed, table, *link_weights),
        scratch=scratch(blocks) + [pltpu.VMEM((width, nodes), F32)],
        flops=4 * 10**9,
        moved=4 * 1024 * 1024,
    )
    near_back = lax.ppermute(near, ("band", "ch"), to_patch)
    own = call(
        functools.partial(own_pool_body, nodes, slots),
        shape((width, nodes), BF16),
        (near, packed, table, *link_weights),
        scratch=scratch(blocks // 2) + [pltpu.VMEM((width, nodes // 2), F32)],
        flops=4 * 10**9,
        moved=4 * 1024 * 1024,
    )
    own_other = other(own)
    near_back_other = other(near_back)

    lanes = lambda a: a.reshape(1, edges)
    mid, rows = call(
        middle_body,
        (
            shape((nodes, width), BF16),
            shape((edges, width), BF16),
        ),
        (
            *(packed, near_back, near_back_other, own, own_other),
            *(link_out, other(*after(near, link_out)), request),
        ),
    )
    late_other = pin(other(*after(mid, late)))
    rows = lax.all_to_all(rows, "band", 0, 0, tiled=True)
    receivers = lanes(mesh_receivers)
    limit = lanes(
        mesh_counts.reshape(bands, 1) - jnp.arange(capacity, dtype=jnp.int32)[None, :]
    )
    base, upper, last_own, last_other = call(
        base_body,
        (
            shape((edges, width), F32),
            shape((nodes, width), F32),
            *[shape((4 * width, half), BF16)] * 2,
        ),
        (mid, receivers, mesh_feats, edge_own, edge_other, pin(late), late_other),
        in_specs=[vmem] * 5 + [hbm] * 2,
        out_specs=(vmem,) * 4,
        scratch=[pltpu.VMEM((2 * width, half), BF16)] * 2 + [pltpu.SemaphoreType.DMA((4,))],
    )
    return call(
        node_body,
        shape((nodes, half), BF16),
        (
            *(rows, base, upper, mid, receivers, limit, norm_gain.reshape(1, half)),
            *(last_own, last_other),
        ),
    )


def solution(mesh):
    rows = P(("grp", "band"), None)
    columns = P(None, ("grp", "band"))
    split = P(("grp", "band"), "ch")
    by_column = P(None, "ch")
    by_row = P("ch", None)
    in_specs = (
        rows,
        rows,
        P(("grp", "band")),
        columns,
        split,
        rows,
        rows,
        rows,
        columns,
        by_column,
        by_row,
        by_column,
        by_column,
        by_column,
        by_row,
        by_column,
        by_column,
        by_column,
        by_row,
        by_column,
        by_row,
        P("ch"),
    )
    return jax.shard_map(
        per_device, mesh=mesh, in_specs=in_specs, out_specs=split, check_vma=False
    )
```
